128 devices in a mesh: patch: 4 (over x_hi, core), epoch: 32 (over z, x_lo, y).
Axes of the slice: x: 4 (x_hi: 2, x_lo: 2; x = x_hi * 2 + x_lo), y: 4, z: 4, core: 2. Of those that a mesh axis runs over, the one named last changes fastest.
Arguments:
- images: bfloat16 [384, 512, 4096], P('epoch', None, 'patch'), may hold values from -8 to 8
- counts: int32 [4, 32], P('patch', 'epoch'), may hold values from 1 to 12, as said below
- slot_weight: float32 [4, 384], P('patch', 'epoch'), may hold values from 0.2 to 5
- kernel_index: int32 [4, 384, 3], P('patch', 'epoch'), may hold values from 0 to 7
- kernel_slope: float32 [4, 384], P('patch', 'epoch'), may hold values from -1 to 1
- tap_basis: float32 [8, 21], replicated, may hold values from 0 to 0.1
Outputs:
- template: bfloat16 [512, 4096], P(None, 'patch')
- differences: bfloat16 [384, 512, 4096], P('epoch', None, 'patch')
The draws below stay inside these ranges and needn't reach their ends.
Inputs may be any that keep to these rules, and one draw needn't show every extreme that they name: `counts`: slots e with e mod 12 >= the holder's count are empty; in every patch some holder uses all 12 slots.
All inputs are finite; a program needn't handle non-finite values.
Results may differ from the reference program's by a relative error of at most 0.0022.
Values may be sent and summed in bfloat16 or wider, within the bound.
No kernel may reach another device: no remote copies, remote signals or barrier semaphores. Data moves between devices by JAX's collectives and lax.ppermute only.
A program may use at most 128 MiB of HBM per device.

```python
import math
import jax
import jax.numpy as jnp
from jax import lax

H = 512
PATCH_W = 1024
EP_DEV = 12
TAPS = 21
NB = 8
STRIP_W = 4096
EPOCHS = 384
N_PATCH = 4
N_EPOCH = 32


def draw_counts(key, part):
    key = jax.random.fold_in(key, 7)
    first, second = jax.random.split(key)
    top = max(2, 2 * EP_DEV // 3)
    values = jax.random.randint(first, (N_PATCH, N_EPOCH), 1, top)
    fullest = jax.random.randint(second, (N_PATCH,), 0, N_EPOCH)
    hit = jnp.arange(N_EPOCH)[None, :] == fullest[:, None]
    return jnp.where(hit, EP_DEV, values).astype(jnp.int32)


def draw_images(key, part):
    key = jax.random.fold_in(key, 11)
    sky_key, noise_key = jax.random.split(key, 2)
    sky = jax.random.normal(sky_key, (H, STRIP_W), jnp.float32)
    noise = jax.random.normal(noise_key, (EPOCHS, H, STRIP_W), jnp.float32)
    return jnp.clip(sky[None, :, :] + noise, -8.0, 8.0).astype(jnp.bfloat16)


def set_ends(drawn, own_key, low, top_value):
    dims = drawn.shape
    spot = [jax.random.randint(jax.random.fold_in(own_key, axis), (), 0, dims[axis]) for axis in range(len(dims))]
    drawn = drawn.at[tuple(spot)].set(low)
    longest = dims.index(max(dims))
    spot[longest] = (spot[longest] + 1) % dims[longest]
    return drawn.at[tuple(spot)].set(top_value)


def shard_levels(stream_key, shape, cuts, least, high):
    loudness = 1.0
    for axis_at, parts in cuts:
        steps = jax.random.uniform(jax.random.fold_in(jax.random.fold_in(stream_key, 6), axis_at), (parts,), jnp.float32, least / len(cuts), high / len(cuts))
        loudness = loudness * jnp.repeat(jnp.exp(steps), shape[axis_at] // parts).reshape((-1,) + (1,) * (len(shape) - 1 - axis_at))
    return loudness


def setup_inputs(seed: int = 0) -> dict:
    arg_keys = jax.random.split(jax.random.key(seed), 7)
    images = draw_images(jax.random.fold_in(arg_keys[6], 71), 0)
    counts = draw_counts(jax.random.fold_in(arg_keys[6], 71), 0)
    slot_weight = jnp.clip(jnp.exp(math.log(5.0) - 3.218876 * jax.random.uniform(arg_keys[2], (N_PATCH, EPOCHS), jnp.float32) ** shard_levels(arg_keys[2], (N_PATCH, EPOCHS), ((0, 4), (1, 32)), -0.2, 0.2)), 0.2, 5.0)
    kernel_index = set_ends(jax.random.randint(arg_keys[3], (N_PATCH, EPOCHS, 3), 0, NB), jax.random.fold_in(arg_keys[3], 1), 0, NB - 1).astype(jnp.int32)
    kernel_slope = jnp.clip(jax.random.uniform(arg_keys[4], (N_PATCH, EPOCHS), jnp.float32, -1.0, 1.0) * shard_levels(arg_keys[4], (N_PATCH, EPOCHS), ((0, 4), (1, 32)), -0.4, 0.0), -1.0, 1.0)
    tap_basis = jnp.clip(jax.random.uniform(arg_keys[5], (NB, TAPS), jnp.float32, 0.0, 0.1), 0.0, 0.1)
    return {"images": images, "counts": counts, "slot_weight": slot_weight, "kernel_index": kernel_index, "kernel_slope": kernel_slope, "tap_basis": tap_basis}


def reference(images, counts, slot_weight, kernel_index, kernel_slope, tap_basis):
    f32 = jnp.float32
    slot_ids = jnp.arange(EPOCHS)
    holder = slot_ids // EP_DEV
    live = (slot_ids % EP_DEV)[None, :] < counts[:, holder]
    live_weight = jnp.where(live, slot_weight, 0.0).astype(f32)
    total_weight = jnp.sum(live_weight, axis=1)
    column_weight = jnp.repeat(live_weight, PATCH_W, axis=0).T

    def accumulate(carry, item):
        image, weights = item
        return carry + image.astype(f32) * weights[None, :], None

    weighted, unused = lax.scan(accumulate, jnp.zeros((H, STRIP_W), f32), (images, column_weight))
    template = (weighted / jnp.repeat(total_weight, PATCH_W)[None, :]).astype(jnp.bfloat16)
    half = TAPS // 2
    padded = jnp.pad(template.astype(f32), ((half, half), (half, half)))
    windows = jnp.stack([padded[:, p * PATCH_W:p * PATCH_W + PATCH_W + 2 * half] for p in range(N_PATCH)])
    taps = jnp.take(tap_basis, kernel_index, axis=0).astype(jnp.bfloat16)
    taps = lax.optimization_barrier(taps).astype(f32)
    position = ((jnp.arange(STRIP_W).astype(f32) + 0.5 - STRIP_W / 2) / (STRIP_W / 2)).reshape(N_PATCH, PATCH_W)

    def one_slot(item):
        image, tap_set, slope, alive = item
        vertical = jnp.zeros((N_PATCH, H, PATCH_W + 2 * half), f32)
        for tap in range(TAPS):
            vertical = vertical + tap_set[:, 0, tap, None, None] * windows[:, tap:tap + H, :]
        vertical = lax.optimization_barrier(vertical.astype(jnp.bfloat16)).astype(f32)
        flat = jnp.zeros((N_PATCH, H, PATCH_W), f32)
        slanted = jnp.zeros((N_PATCH, H, PATCH_W), f32)
        for tap in range(TAPS):
            piece = vertical[:, :, tap:tap + PATCH_W]
            flat = flat + tap_set[:, 1, tap, None, None] * piece
            slanted = slanted + tap_set[:, 2, tap, None, None] * piece
        matched = flat + slope[:, None, None] * position[:, None, :] * slanted
        local = image.astype(f32).reshape(H, N_PATCH, PATCH_W).transpose(1, 0, 2)
        result = jnp.where(alive[:, None, None], local - matched, 0.0)
        return result.transpose(1, 0, 2).reshape(H, STRIP_W).astype(jnp.bfloat16)

    differences = lax.map(one_slot, (images, taps.transpose(1, 0, 2, 3), kernel_slope.T, live.T))
    return template, differences
```

```python
import functools
import jax, jax.numpy as jnp
from jax import lax
from jax.experimental import pallas as pl
from jax.experimental.pallas import tpu as pltpu
from jax.sharding import PartitionSpec as P
f32=jnp.float32; bf16=jnp.bfloat16
TAPS=21; HALF=10; LANE=128; ROWOFF=16; COLOFF=16

def bands_kernel(idx_ref, basis_ref, a_ref, b_ref, *, slots):
    d_a = lax.broadcasted_iota(jnp.int32,(128,256),1)-lax.broadcasted_iota(jnp.int32,(128,256),0)-(ROWOFF-HALF)
    d_b = lax.broadcasted_iota(jnp.int32,(256,128),0)-lax.broadcasted_iota(jnp.int32,(256,128),1)-(COLOFF-HALF)
    def body(s,_):
        ia=idx_ref[s,0]; i1=idx_ref[s,1]; i2=idx_ref[s,2]
        a=jnp.zeros((128,256),f32); b1=jnp.zeros((256,128),f32); b2=jnp.zeros((256,128),f32)
        for t in range(TAPS):
            a=jnp.where(d_a==t, basis_ref[ia,t], a)
            m=d_b==t
            b1=jnp.where(m, basis_ref[i1,t], b1)
            b2=jnp.where(m, basis_ref[i2,t], b2)
        a_ref[s]=a.astype(bf16)
        b_ref[s,:,0:128]=b1.astype(bf16)
        b_ref[s,:,128:256]=b2.astype(bf16)
        return 0
    lax.fori_loop(0,slots,body,0)

def bands(idx, basis):
    slots=idx.shape[0]
    return pl.pallas_call(functools.partial(bands_kernel,slots=slots),
        out_shape=(jax.ShapeDtypeStruct((slots,128,256),bf16),jax.ShapeDtypeStruct((slots,256,256),bf16)),
        in_specs=[pl.BlockSpec(memory_space=pltpu.SMEM)]*2,
        out_specs=(pl.BlockSpec(memory_space=pltpu.VMEM),)*2,
        compiler_params=pltpu.CompilerParams(vmem_limit_bytes=40*2**20),
        name="bands")(idx,basis)


def acc_kernel(count_ref, w_ref, img_ref, out_ref, *, slots, chunk_rows):
    total = None
    weight = 0.0
    for s in range(slots):
        wt = jnp.where(s < count_ref[0, 0], w_ref[0, s], 0.0)
        weight = weight + wt
        v = img_ref[s].astype(f32) * wt
        total = v if total is None else total + v
    rows, width = total.shape
    cols = width // LANE
    stride = (chunk_rows // 8 * cols + 1) * 8
    for q in range(rows // chunk_rows):
        for r in range(chunk_rows // 8):
            for c in range(cols):
                at = q * stride + (r * cols + c) * 8
                row = q * chunk_rows + r * 8
                out_ref[at : at + 8, :] = total[row : row + 8, c * LANE : (c + 1) * LANE]
        out_ref[(q + 1) * stride - 8 : (q + 1) * stride, :] = jnp.full((8, LANE), weight, f32)


def accumulate(counts, w, images, chunk_rows, rb=32):
    slots, rows, width = images.shape
    stride = (chunk_rows * width // LANE) + 8
    per = rb // chunk_rows
    return pl.pallas_call(
        functools.partial(acc_kernel, slots=slots, chunk_rows=chunk_rows),
        grid=(rows // rb,),
        out_shape=jax.ShapeDtypeStruct((rows // chunk_rows * stride, LANE), f32),
        in_specs=[pl.BlockSpec(memory_space=pltpu.SMEM)] * 2
        + [pl.BlockSpec((slots, rb, width), lambda i: (0, i, 0))],
        out_specs=pl.BlockSpec((per * stride, LANE), lambda i: (i, 0)),
        compiler_params=pltpu.CompilerParams(vmem_limit_bytes=40 * 2**20),
        name="accumulate",
    )(counts, w, images)


def share_kernel(x_ref, out_ref, *, parts, chunk_rows, width):
    total = x_ref[0]
    for p in range(1, parts):
        total = total + x_ref[p]
    cols = width // LANE
    tiles = chunk_rows // 8 * cols
    weight = total[tiles * 8 : tiles * 8 + 8, :]
    bands_of = []
    for r in range(chunk_rows // 8):
        bands_of.append(
            jnp.concatenate(
                [total[(r * cols + c) * 8 : (r * cols + c) * 8 + 8, :] / weight for c in range(cols)], axis=1
            )
        )
    own = jnp.concatenate(bands_of, axis=0).astype(bf16)
    for p in range(parts):
        out_ref[p] = own


def share(x, parts, chunk_rows, width):
    return pl.pallas_call(
        functools.partial(share_kernel, parts=parts, chunk_rows=chunk_rows, width=width),
        out_shape=jax.ShapeDtypeStruct((parts, chunk_rows, width), bf16),
        in_specs=[pl.BlockSpec(memory_space=pltpu.VMEM)],
        out_specs=pl.BlockSpec(memory_space=pltpu.VMEM),
        compiler_params=pltpu.CompilerParams(vmem_limit_bytes=40 * 2**20),
        name="share",
    )(x)


def match_kernel(count_ref, slope_ref, pos_ref, t_ref, lo_ref, hi_ref, a_ref, b_ref, img_ref, out_ref, tp, v, *, slots, width, rows, variant):
    n=pl.program_id(0)
    tiles=width//LANE
    @pl.when(n==0)
    def _():
        z=jnp.zeros((ROWOFF,width+LANE),bf16)
        tp[0:ROWOFF,:]=z
        tp[ROWOFF+rows:ROWOFF+rows+128-ROWOFF,:]=jnp.zeros((128-ROWOFF,width+LANE),bf16)
        for r in range(0,rows,64):
            prev=lo_ref[r:r+64,:].astype(f32)
            prev=pltpu.roll(prev,COLOFF,1)
            lane=lax.broadcasted_iota(jnp.int32,(64,LANE),1)
            for c in range(tiles+1):
                cur = t_ref[r:r+64,c*LANE:(c+1)*LANE] if c<tiles else hi_ref[r:r+64,:]
                cur=pltpu.roll(cur.astype(f32),COLOFF,1)
                tp[ROWOFF+r:ROWOFF+r+64,c*LANE:(c+1)*LANE]=jnp.where(lane<COLOFF,prev,cur).astype(bf16)
                prev=cur
    win=tp[pl.ds(pl.multiple_of(n*128,128),256),:]
    A=a_ref[...].reshape(slots*128,256)
    for j in range(0,tiles+1,2):
        w=min(2,tiles+1-j)*LANE
        v[:,j*LANE:j*LANE+w]=jnp.dot(A,win[:,j*LANE:j*LANE+w],preferred_element_type=f32).astype(bf16)
    def slot(s,_):
        r0=pl.multiple_of(s*128,128)
        @pl.when(s<count_ref[0,0])
        def _():
            sl=slope_ref[0,s]
            b=b_ref[s]
            if variant==0:
                for m in range(tiles):
                    o=jnp.dot(v[pl.ds(r0,128),m*LANE:m*LANE+256],b,preferred_element_type=f32)
                    p=pos_ref[0:1,m*LANE:(m+1)*LANE]*sl
                    out_ref[s,:,m*LANE:(m+1)*LANE]=(img_ref[s,:,m*LANE:(m+1)*LANE].astype(f32)-(o[:,:LANE]+p*o[:,LANE:])).astype(bf16)
            else:
                lhs=jnp.concatenate([v[pl.ds(r0,128),m*LANE:m*LANE+256] for m in range(tiles)],axis=0)
                o=jnp.dot(lhs,b,preferred_element_type=f32)
                for m in range(tiles):
                    p=pos_ref[0:1,m*LANE:(m+1)*LANE]*sl
                    oo=o[m*128:(m+1)*128]
                    out_ref[s,:,m*LANE:(m+1)*LANE]=(img_ref[s,:,m*LANE:(m+1)*LANE].astype(f32)-(oo[:,:LANE]+p*oo[:,LANE:])).astype(bf16)
        @pl.when(s>=count_ref[0,0])
        def _():
            out_ref[s]=jnp.zeros(out_ref.shape[1:],bf16)
        return 0
    lax.fori_loop(0,slots,slot,0)

def match(counts, slopes, pos, t, lo, hi, a, b, images, variant=0):
    slots,rows,width=images.shape
    vm=pl.BlockSpec(memory_space=pltpu.VMEM)
    sm=pl.BlockSpec(memory_space=pltpu.SMEM)
    return pl.pallas_call(functools.partial(match_kernel,slots=slots,width=width,rows=rows,variant=variant),
        grid=(rows//128,),
        out_shape=jax.ShapeDtypeStruct(images.shape,bf16),
        in_specs=[sm,sm,vm,vm,vm,vm,vm,vm,pl.BlockSpec((slots,128,width),lambda i:(0,i,0))],
        out_specs=pl.BlockSpec((slots,128,width),lambda i:(0,i,0)),
        scratch_shapes=[pltpu.VMEM((rows+128,width+LANE),bf16),pltpu.VMEM((slots*128,width+LANE),bf16)],
        compiler_params=pltpu.CompilerParams(vmem_limit_bytes=56*2**20),
        cost_estimate=pl.CostEstimate(flops=10**10,bytes_accessed=28*10**6,transcendentals=0),
        name="match")(counts,slopes,pos,t,lo,hi,a,b,images)


def on_device(images, counts, slot_weight, kernel_index, kernel_slope, tap_basis):
    slots, rows, width = images.shape
    parts = lax.axis_size("epoch")
    patches = lax.axis_size("patch")
    chunk_rows = rows // parts
    partial = accumulate(counts, slot_weight, images, chunk_rows)
    pieces = lax.all_to_all(partial, "epoch", 0, 0, tiled=True)
    copies = share(pieces.reshape(parts, -1, LANE), parts, chunk_rows, width)
    template = lax.all_to_all(copies, "epoch", 0, 0, tiled=True).reshape(rows, width)
    forward = [(i, i + 1) for i in range(patches - 1)]
    backward = [(i + 1, i) for i in range(patches - 1)]
    low = lax.ppermute(template[:, width - LANE :], "patch", forward)
    high = lax.ppermute(template[:, :LANE], "patch", backward)
    a, b = bands(kernel_index[0], tap_basis)
    columns = lax.axis_index("patch") * width + jnp.arange(width)
    center = width * patches / 2
    position = ((columns.astype(f32) + 0.5 - center) / center).reshape(1, width)
    differences = match(counts, kernel_slope, position, template, low, high, a, b, images)
    return (template, differences)


def solution(mesh):
    in_specs = (
        P("epoch", None, "patch"),
        P("patch", "epoch"),
        P("patch", "epoch"),
        P("patch", "epoch", None),
        P("patch", "epoch"),
        P(),
    )
    out_specs = (P(None, "patch"), P("epoch", None, "patch"))
    return jax.shard_map(
        on_device, mesh=mesh, in_specs=in_specs, out_specs=out_specs, check_vma=False
    )
```

```python
import functools

import jax
import jax.numpy as jnp
from jax import lax
from jax.experimental import pallas as pl
from jax.experimental.pallas import tpu as pltpu
from jax.sharding import PartitionSpec as P

f32 = jnp.float32
bf16 = jnp.bfloat16
LANE = 128
PAD = 16
VMEM_LIMIT = 44 * 2**20


def smem():
    return pl.BlockSpec(memory_space=pltpu.SMEM)


def vmem():
    return pl.BlockSpec(memory_space=pltpu.VMEM)


def params():
    return pltpu.CompilerParams(vmem_limit_bytes=VMEM_LIMIT)


def bands_kernel(index_ref, basis_ref, vert_ref, horiz_ref, *, slots, taps):
    lead = PAD - taps // 2
    lane = lax.broadcasted_iota(jnp.int32, (8, 2 * LANE), 1)

    def body(s, _):
        first, second, third = index_ref[s, 0], index_ref[s, 1], index_ref[s, 2]
        row0 = jnp.zeros((8, 2 * LANE), f32)
        row1 = jnp.zeros((8, 2 * LANE), f32)
        row2 = jnp.zeros((8, 2 * LANE), f32)
        for t in range(taps):
            row0 = jnp.where(lane == lead + t, basis_ref[first, t], row0)
            back = lane == 2 * LANE - lead - t
            row1 = jnp.where(back, basis_ref[second, t], row1)
            row2 = jnp.where(back, basis_ref[third, t], row2)
        row2 = jnp.concatenate([row2[:, LANE:], row2[:, :LANE]], axis=1)
        for base in range(0, 2 * LANE, 16):
            if base < LANE:
                halves = [pltpu.roll(row0, base + 8 * h, 1, stride=1, stride_axis=0) for h in range(2)]
                vert_ref[s, base : base + 16, :] = jnp.concatenate(halves, axis=0).astype(bf16)
            halves = []
            for h in range(2):
                r1 = pltpu.roll(row1, base + 8 * h, 1, stride=1, stride_axis=0)
                r2 = pltpu.roll(row2, base + 8 * h, 1, stride=1, stride_axis=0)
                halves.append(jnp.concatenate([r1[:, :LANE], r2[:, LANE:]], axis=1))
            horiz_ref[s, base : base + 16, :] = jnp.concatenate(halves, axis=0).astype(bf16)
        return 0

    lax.fori_loop(0, slots, body, 0)


def tap_bands(index, basis):
    slots = index.shape[0]
    return pl.pallas_call(
        functools.partial(bands_kernel, slots=slots, taps=basis.shape[1]),
        out_shape=(
            jax.ShapeDtypeStruct((slots, LANE, 2 * LANE), bf16),
            jax.ShapeDtypeStruct((slots, 2 * LANE, 2 * LANE), bf16),
        ),
        in_specs=[smem(), smem()],
        out_specs=(vmem(), vmem()),
        compiler_params=params(),
        name="tap_bands",
    )(index, basis)


def accumulate_kernel(count_ref, weight_ref, image_ref, out_ref, *, slots, chunk):
    weights = [jnp.where(s < count_ref[0, 0], weight_ref[0, s], 0.0) for s in range(slots)]
    total = weights[0]
    for s in range(1, slots):
        total = total + weights[s]
    rows, width = image_ref.shape[1:]
    cols = width // LANE
    stride = (chunk // 8 * cols + 1) * 8
    for q in range(rows // chunk):
        for r in range(chunk // 16):
            for c in range(cols):
                at = slice(c * LANE, (c + 1) * LANE)
                row = q * chunk + r * 16
                part = image_ref[0, row : row + 16, at].astype(f32) * weights[0]
                for s in range(1, slots):
                    part = part + image_ref[s, row : row + 16, at].astype(f32) * weights[s]
                for h in range(2):
                    base = q * stride + ((2 * r + h) * cols + c) * 8
                    out_ref[base : base + 8, :] = part[8 * h : 8 * h + 8]
        out_ref[(q + 1) * stride - 8 : (q + 1) * stride, :] = jnp.full((8, LANE), total, f32)


def accumulate(counts, weight, images, chunk, block=64):
    slots, rows, width = images.shape
    stride = chunk * width // LANE + 8
    return pl.pallas_call(
        functools.partial(accumulate_kernel, slots=slots, chunk=chunk),
        grid=(rows // block,),
        out_shape=jax.ShapeDtypeStruct((rows // chunk * stride, LANE), f32),
        in_specs=[smem(), smem(), pl.BlockSpec((slots, block, width), lambda i: (0, i, 0))],
        out_specs=pl.BlockSpec((block // chunk * stride, LANE), lambda i: (i, 0)),
        compiler_params=params(),
        name="accumulate",
    )(counts, weight, images)


def share_kernel(piece_ref, own_ref, first_ref, last_ref, *, parts, chunk, width):
    cols = width // LANE
    tiles = chunk // 8 * cols
    weight = piece_ref[0, tiles * 8 :, :]
    for p in range(1, parts):
        weight = weight + piece_ref[p, tiles * 8 :, :]
    for r in range(chunk // 16):
        for c in range(cols):
            halves = []
            for h in range(2):
                base = ((2 * r + h) * cols + c) * 8
                total = piece_ref[0, base : base + 8, :]
                for p in range(1, parts):
                    total = total + piece_ref[p, base : base + 8, :]
                halves.append(total / weight)
            block = jnp.concatenate(halves, axis=0).astype(bf16)
            own_ref[16 * r : 16 * r + 16, c * LANE : (c + 1) * LANE] = block
            if c == 0:
                first_ref[16 * r : 16 * r + 16, :] = block
            if c == cols - 1:
                last_ref[16 * r : 16 * r + 16, :] = block


def share(pieces, chunk, width):
    parts = pieces.shape[0]
    return pl.pallas_call(
        functools.partial(share_kernel, parts=parts, chunk=chunk, width=width),
        out_shape=(
            jax.ShapeDtypeStruct((chunk, width), bf16),
            jax.ShapeDtypeStruct((chunk, LANE), bf16),
            jax.ShapeDtypeStruct((chunk, LANE), bf16),
        ),
        in_specs=[vmem()],
        out_specs=(vmem(), vmem(), vmem()),
        compiler_params=params(),
        name="share",
    )(pieces)


def widen_kernel(own_ref, low_ref, high_ref, out_ref, *, parts):
    rows, width = own_ref.shape
    cols = width // LANE
    lane = lax.broadcasted_iota(jnp.int32, (rows, LANE), 1)
    before = pltpu.roll(low_ref[...].astype(f32), PAD, 1)
    for c in range(cols + 1):
        here = own_ref[:, c * LANE : (c + 1) * LANE] if c < cols else high_ref[...]
        here = pltpu.roll(here.astype(f32), PAD, 1)
        block = jnp.where(lane < PAD, before, here).astype(bf16)
        for p in range(parts):
            out_ref[p, :, c * LANE : (c + 1) * LANE] = block
        before = here


def widen(own, low, high, parts):
    rows, width = own.shape
    return pl.pallas_call(
        functools.partial(widen_kernel, parts=parts),
        out_shape=jax.ShapeDtypeStruct((parts, rows, width + LANE), bf16),
        in_specs=[vmem()] * 3,
        out_specs=vmem(),
        compiler_params=params(),
        name="widen",
    )(own, low, high)


def match_kernel(
    count_ref, slope_ref, wide_ref, vert_ref, horiz_ref, image_ref, diff_ref, template_ref, padded, vertical, *, group
):
    step = pl.program_id(0)
    rows, width = image_ref.shape[1:]
    cols = width // LANE
    count = count_ref[0, 0]

    @pl.when(step == 0)
    def _():
        padded[0:PAD, :] = jnp.zeros((PAD, width + LANE), bf16)
        padded[PAD + rows :, :] = jnp.zeros((LANE - PAD, width + LANE), bf16)
        padded[PAD : PAD + rows, :] = wide_ref[...]

    @pl.when(step < rows // LANE)
    def _():
        lane = lax.broadcasted_iota(jnp.int32, (LANE, LANE), 1)
        at = pl.ds(pl.multiple_of(step * LANE, LANE), LANE)
        here = pltpu.roll(wide_ref[at, :LANE].astype(f32), LANE - PAD, 1)
        for c in range(cols):
            after = pltpu.roll(wide_ref[at, (c + 1) * LANE : (c + 2) * LANE].astype(f32), LANE - PAD, 1)
            template_ref[:, c * LANE : (c + 1) * LANE] = jnp.where(lane < LANE - PAD, here, after).astype(bf16)
            here = after

    @pl.when(step * group < count)
    def _():
        band = vert_ref[...].reshape(group * LANE, 2 * LANE)
        for n in range(rows // LANE):
            for j in range(0, cols + 1, 2):
                at = slice(j * LANE, min(j + 2, cols + 1) * LANE)
                part = jnp.dot(band, padded[n * LANE : (n + 2) * LANE, at], preferred_element_type=f32).astype(bf16)
                for g in range(group):
                    vertical[g, n * LANE : (n + 1) * LANE, at] = part[g * LANE : (g + 1) * LANE]
        start = lax.axis_index("patch") * width
        center = width * lax.axis_size("patch") / 2
        column = lax.broadcasted_iota(jnp.int32, (8, LANE), 1) + start
        for g in range(group):
            slot = step * group + g
            live = slot < count
            slope = slope_ref[0, slot]
            for m in range(cols):
                at = slice(m * LANE, (m + 1) * LANE)
                position = ((column + m * LANE).astype(f32) + 0.5 - center) / center
                factor = (slope * position)[0:1]
                both = jnp.dot(vertical[g, :, m * LANE : (m + 2) * LANE], horiz_ref[g], preferred_element_type=f32)
                matched = both[:, :LANE] + factor * both[:, LANE:]
                result = jnp.where(live, image_ref[g, :, at].astype(f32) - matched, 0.0)
                diff_ref[g, :, at] = result.astype(bf16)

    @pl.when(step * group >= count)
    def _():
        diff_ref[...] = jnp.zeros(diff_ref.shape, bf16)


def match(counts, slopes, wide, vert, horiz, images, group=2):
    slots, rows, width = images.shape
    last = rows // LANE - 1
    return pl.pallas_call(
        functools.partial(match_kernel, group=group),
        grid=(slots // group,),
        out_shape=(jax.ShapeDtypeStruct(images.shape, bf16), jax.ShapeDtypeStruct((rows, width), bf16)),
        in_specs=[
            smem(),
            smem(),
            vmem(),
            pl.BlockSpec((group, LANE, 2 * LANE), lambda i: (i, 0, 0)),
            pl.BlockSpec((group, 2 * LANE, 2 * LANE), lambda i: (i, 0, 0)),
            pl.BlockSpec((group, rows, width), lambda i: (i, 0, 0)),
        ],
        out_specs=(
            pl.BlockSpec((group, rows, width), lambda i: (i, 0, 0)),
            pl.BlockSpec((LANE, width), lambda i: (jnp.minimum(i, last), 0)),
        ),
        scratch_shapes=[
            pltpu.VMEM((rows + LANE, width + LANE), bf16),
            pltpu.VMEM((group, rows, width + LANE), bf16),
        ],
        compiler_params=params(),
        name="match",
    )(counts, slopes, wide, vert, horiz, images)


def on_device(images, counts, slot_weight, kernel_index, kernel_slope, tap_basis):
    slots, rows, width = images.shape
    parts = lax.axis_size("epoch")
    patches = lax.axis_size("patch")
    chunk = rows // parts
    partial = accumulate(counts, slot_weight, images, chunk)
    pieces = lax.all_to_all(partial, "epoch", 0, 0, tiled=True)
    own, first, last = share(pieces.reshape(parts, -1, LANE), chunk, width)
    low = lax.ppermute(last, "patch", [(i, i + 1) for i in range(patches - 1)])
    high = lax.ppermute(first, "patch", [(i + 1, i) for i in range(patches - 1)])
    vert, horiz = tap_bands(kernel_index[0], tap_basis)
    copies = widen(own, low, high, parts)
    wide = lax.all_to_all(copies, "epoch", 0, 0, tiled=True).reshape(rows, width + LANE)
    differences, template = match(counts, kernel_slope, wide, vert, horiz, images)
    return (template, differences)


def solution(mesh):
    in_specs = (
        P("epoch", None, "patch"),
        P("patch", "epoch"),
        P("patch", "epoch"),
        P("patch", "epoch", None),
        P("patch", "epoch"),
        P(),
    )
    out_specs = (P(None, "patch"), P("epoch", None, "patch"))
    return jax.shard_map(
        on_device, mesh=mesh, in_specs=in_specs, out_specs=out_specs, check_vma=False
    )
```

```python
import functools

import jax
import jax.numpy as jnp
from jax import lax
from jax.experimental import pallas as pl
from jax.experimental.pallas import tpu as pltpu
from jax.sharding import PartitionSpec as P

f32 = jnp.float32
bf16 = jnp.bfloat16
LANE = 128
RING = 4
PAD = 16
VMEM_LIMIT = 44 * 2**20


def smem():
    return pl.BlockSpec(memory_space=pltpu.SMEM)


def vmem():
    return pl.BlockSpec(memory_space=pltpu.VMEM)


def params():
    return pltpu.CompilerParams(vmem_limit_bytes=VMEM_LIMIT)


def bands_kernel(index_ref, basis_ref, vert_ref, horiz_ref, *, slots, taps):
    lead = PAD - taps // 2
    lane = lax.broadcasted_iota(jnp.int32, (8, 2 * LANE), 1)

    def body(s, _):
        first, second, third = index_ref[s, 0], index_ref[s, 1], index_ref[s, 2]
        row0 = jnp.zeros((8, 2 * LANE), f32)
        row1 = jnp.zeros((8, 2 * LANE), f32)
        row2 = jnp.zeros((8, 2 * LANE), f32)
        for t in range(taps):
            row0 = jnp.where(lane == lead + t, basis_ref[first, t], row0)
            back = lane == 2 * LANE - lead - t
            row1 = jnp.where(back, basis_ref[second, t], row1)
            row2 = jnp.where(back, basis_ref[third, t], row2)
        row2 = jnp.concatenate([row2[:, LANE:], row2[:, :LANE]], axis=1)
        for base in range(0, 2 * LANE, 16):
            if base < LANE:
                halves = [pltpu.roll(row0, base + 8 * h, 1, stride=1, stride_axis=0) for h in range(2)]
                vert_ref[s, base : base + 16, :] = jnp.concatenate(halves, axis=0).astype(bf16)
            halves = []
            for h in range(2):
                r1 = pltpu.roll(row1, base + 8 * h, 1, stride=1, stride_axis=0)
                r2 = pltpu.roll(row2, base + 8 * h, 1, stride=1, stride_axis=0)
                halves.append(jnp.concatenate([r1[:, :LANE], r2[:, LANE:]], axis=1))
            horiz_ref[s, base : base + 16, :] = jnp.concatenate(halves, axis=0).astype(bf16)
        return 0

    lax.fori_loop(0, slots, body, 0)


def tap_bands(index, basis):
    slots = index.shape[0]
    return pl.pallas_call(
        functools.partial(bands_kernel, slots=slots, taps=basis.shape[1]),
        out_shape=(
            jax.ShapeDtypeStruct((slots, LANE, 2 * LANE), bf16),
            jax.ShapeDtypeStruct((slots, 2 * LANE, 2 * LANE), bf16),
        ),
        in_specs=[smem(), smem()],
        out_specs=(vmem(), vmem()),
        compiler_params=params(),
        name="tap_bands",
    )(index, basis)


def place():
    index = lax.axis_index("epoch")
    return index // (RING * 2), index // RING % 2, index % RING


def moves(step):
    pairs = []
    for index in range(2 * RING * RING):
        z, x, y = step(index // (RING * 2), index // RING % 2, index % RING)
        pairs.append((index, (z % RING * 2 + x % 2) * RING + y % RING))
    return pairs


def chunk_sum(image_ref, weights, total, out_ref):
    slots, rows, width = image_ref.shape
    cols = width // LANE
    for r in range(rows // 16):
        for c in range(cols):
            at = slice(c * LANE, (c + 1) * LANE)
            part = image_ref[0, 16 * r : 16 * r + 16, at].astype(f32) * weights[0]
            for s in range(1, slots):
                part = part + image_ref[s, 16 * r : 16 * r + 16, at].astype(f32) * weights[s]
            for h in range(2):
                base = ((2 * r + h) * cols + c) * 8
                out_ref[base : base + 8, :] = part[8 * h : 8 * h + 8]
    out_ref[rows * cols :, :] = jnp.full((8, LANE), total, f32)


def accumulate_kernel(count_ref, weight_ref, image_ref, *refs, shifts, chunk):
    outs, (held, arrived) = refs[:-2], refs[-2:]
    slots, rows, _ = image_ref.shape
    z, _, y = place()
    copies = []
    for i, shift in enumerate(shifts):
        for half, at in enumerate((z, y)):
            start = pl.multiple_of(half * (rows // 2) + lax.rem(at + shift, RING) * chunk, chunk)
            n = 2 * i + half
            copy = pltpu.make_async_copy(image_ref.at[:, pl.ds(start, chunk), :], held.at[n], arrived.at[n])
            copy.start()
            copies.append(copy)
    weights = [jnp.where(s < count_ref[0, 0], weight_ref[0, s], 0.0) for s in range(slots)]
    total = weights[0]
    for s in range(1, slots):
        total = total + weights[s]
    for n, copy in enumerate(copies):
        copy.wait()
        chunk_sum(held.at[n], weights, total, outs[n])


def accumulate(counts, weight, images, shifts):
    slots, rows, width = images.shape
    chunk = rows // (2 * RING)
    count = 2 * len(shifts)
    return pl.pallas_call(
        functools.partial(accumulate_kernel, shifts=shifts, chunk=chunk),
        out_shape=(jax.ShapeDtypeStruct((chunk * width // LANE + 8, LANE), f32),) * count,
        in_specs=[smem(), smem(), pl.BlockSpec(memory_space=pl.ANY)],
        out_specs=(vmem(),) * count,
        scratch_shapes=[pltpu.VMEM((count, slots, chunk, width), bf16), pltpu.SemaphoreType.DMA((count,))],
        cost_estimate=pl.CostEstimate(
            flops=count * slots * chunk * width * 2, bytes_accessed=count * slots * chunk * width * 2, transcendentals=0
        ),
        compiler_params=params(),
        name="accumulate",
    )(counts, weight, images)


def fold_kernel(*refs):
    ins, (keep_ref, send_ref) = refs[:-2], refs[-2:]
    upper = ins[0][...]
    lower = ins[1][...]
    for i in range(2, len(ins), 2):
        upper = upper + ins[i][...]
        lower = lower + ins[i + 1][...]
    _, x, _ = place()

    @pl.when(x == 0)
    def _():
        keep_ref[...] = upper
        send_ref[...] = lower

    @pl.when(x == 1)
    def _():
        keep_ref[...] = lower
        send_ref[...] = upper


def fold(parts):
    shape = jax.ShapeDtypeStruct(parts[0].shape, f32)
    return pl.pallas_call(
        fold_kernel,
        out_shape=(shape, shape),
        in_specs=[vmem()] * len(parts),
        out_specs=(vmem(), vmem()),
        compiler_params=params(),
        name="fold",
    )(*parts)


def cut_kernel(keep_ref, got_ref, *outs):
    rows = outs[0].shape[0] - 8
    z, x, y = place()
    at = jnp.where(x == 0, y, z)
    weight = keep_ref[rows * RING :, :] + got_ref[rows * RING :, :]
    for shift, out_ref in enumerate(outs):
        start = pl.multiple_of(lax.rem(at + shift, RING) * rows, rows)
        out_ref[:rows, :] = keep_ref[pl.ds(start, rows), :] + got_ref[pl.ds(start, rows), :]
        out_ref[rows:, :] = weight


def cut(keep, got):
    rows = (keep.shape[0] - 8) // RING + 8
    return pl.pallas_call(
        cut_kernel,
        out_shape=(jax.ShapeDtypeStruct((rows, LANE), f32),) * RING,
        in_specs=[vmem(), vmem()],
        out_specs=(vmem(),) * RING,
        compiler_params=params(),
        name="cut",
    )(keep, got)


def share_kernel(*refs):
    pieces, (own_ref, first_ref, last_ref) = refs[:-3], refs[-3:]
    chunk, width = own_ref.shape
    cols = width // LANE
    tiles = chunk // 8 * cols
    total = pieces[0][...]
    for piece in pieces[1:]:
        total = total + piece[...]
    weight = total[tiles * 8 :]
    for r in range(chunk // 16):
        for c in range(cols):
            halves = []
            for h in range(2):
                base = ((2 * r + h) * cols + c) * 8
                halves.append(total[base : base + 8] / weight)
            block = jnp.concatenate(halves, axis=0).astype(bf16)
            own_ref[16 * r : 16 * r + 16, c * LANE : (c + 1) * LANE] = block
            if c == 0:
                first_ref[16 * r : 16 * r + 16, :] = block
            if c == cols - 1:
                last_ref[16 * r : 16 * r + 16, :] = block


def share(pieces, chunk, width):
    return pl.pallas_call(
        share_kernel,
        out_shape=(
            jax.ShapeDtypeStruct((chunk, width), bf16),
            jax.ShapeDtypeStruct((chunk, LANE), bf16),
            jax.ShapeDtypeStruct((chunk, LANE), bf16),
        ),
        in_specs=[vmem()] * len(pieces),
        out_specs=(vmem(), vmem(), vmem()),
        compiler_params=params(),
        name="share",
    )(*pieces)


def widen_kernel(own_ref, low_ref, high_ref, out_ref, *, parts):
    rows, width = own_ref.shape
    cols = width // LANE
    lane = lax.broadcasted_iota(jnp.int32, (rows, LANE), 1)
    before = pltpu.roll(low_ref[...].astype(f32), PAD, 1)
    for c in range(cols + 1):
        here = own_ref[:, c * LANE : (c + 1) * LANE] if c < cols else high_ref[...]
        here = pltpu.roll(here.astype(f32), PAD, 1)
        block = jnp.where(lane < PAD, before, here).astype(bf16)
        for p in range(parts):
            out_ref[p, :, c * LANE : (c + 1) * LANE] = block
        before = here


def widen(own, low, high, parts):
    rows, width = own.shape
    return pl.pallas_call(
        functools.partial(widen_kernel, parts=parts),
        out_shape=jax.ShapeDtypeStruct((parts, rows, width + LANE), bf16),
        in_specs=[vmem()] * 3,
        out_specs=vmem(),
        compiler_params=params(),
        name="widen",
    )(own, low, high)


def match_kernel(
    count_ref, slope_ref, wide_ref, vert_ref, horiz_ref, image_ref, diff_ref, template_ref, padded, vertical, *, group
):
    step = pl.program_id(0)
    rows, width = image_ref.shape[1:]
    cols = width // LANE
    count = count_ref[0, 0]

    @pl.when(step == 0)
    def _():
        padded[0:PAD, :] = jnp.zeros((PAD, width + LANE), bf16)
        padded[PAD + rows :, :] = jnp.zeros((LANE - PAD, width + LANE), bf16)
        chunk = wide_ref.shape[1]
        for index in range(wide_ref.shape[0]):
            z, x, y = index // (RING * 2), index // RING % 2, index % RING
            row = PAD + (x * RING * RING + (z * RING + y if x == 0 else y * RING + z)) * chunk
            padded[row : row + chunk, :] = wide_ref[index]

    @pl.when(step < rows // LANE)
    def _():
        lane = lax.broadcasted_iota(jnp.int32, (LANE, LANE), 1)
        at = pl.ds(pl.multiple_of(step * LANE + PAD, PAD), LANE)
        here = pltpu.roll(padded[at, :LANE].astype(f32), LANE - PAD, 1)
        for c in range(cols):
            after = pltpu.roll(padded[at, (c + 1) * LANE : (c + 2) * LANE].astype(f32), LANE - PAD, 1)
            template_ref[:, c * LANE : (c + 1) * LANE] = jnp.where(lane < LANE - PAD, here, after).astype(bf16)
            here = after

    @pl.when(step * group < count)
    def _():
        band = vert_ref[...].reshape(group * LANE, 2 * LANE)
        for n in range(rows // LANE):
            for j in range(0, cols + 1, 2):
                at = slice(j * LANE, min(j + 2, cols + 1) * LANE)
                part = jnp.dot(band, padded[n * LANE : (n + 2) * LANE, at], preferred_element_type=f32).astype(bf16)
                for g in range(group):
                    vertical[g, n * LANE : (n + 1) * LANE, at] = part[g * LANE : (g + 1) * LANE]
        start = lax.axis_index("patch") * width
        center = width * lax.axis_size("patch") / 2
        column = lax.broadcasted_iota(jnp.int32, (8, LANE), 1) + start
        for g in range(group):
            slot = step * group + g
            live = slot < count
            slope = slope_ref[0, slot]
            for m in range(cols):
                at = slice(m * LANE, (m + 1) * LANE)
                position = ((column + m * LANE).astype(f32) + 0.5 - center) / center
                factor = (slope * position)[0:1]
                both = jnp.dot(vertical[g, :, m * LANE : (m + 2) * LANE], horiz_ref[g], preferred_element_type=f32)
                matched = both[:, :LANE] + factor * both[:, LANE:]
                result = jnp.where(live, image_ref[g, :, at].astype(f32) - matched, 0.0)
                diff_ref[g, :, at] = result.astype(bf16)

    @pl.when(step * group >= count)
    def _():
        diff_ref[...] = jnp.zeros(diff_ref.shape, bf16)


def match(counts, slopes, wide, vert, horiz, images, group=2):
    slots, rows, width = images.shape
    last = rows // LANE - 1
    return pl.pallas_call(
        functools.partial(match_kernel, group=group),
        grid=(slots // group,),
        out_shape=(jax.ShapeDtypeStruct(images.shape, bf16), jax.ShapeDtypeStruct((rows, width), bf16)),
        in_specs=[
            smem(),
            smem(),
            vmem(),
            pl.BlockSpec((group, LANE, 2 * LANE), lambda i: (i, 0, 0)),
            pl.BlockSpec((group, 2 * LANE, 2 * LANE), lambda i: (i, 0, 0)),
            pl.BlockSpec((group, rows, width), lambda i: (i, 0, 0)),
        ],
        out_specs=(
            pl.BlockSpec((group, rows, width), lambda i: (i, 0, 0)),
            pl.BlockSpec((LANE, width), lambda i: (jnp.minimum(i, last), 0)),
        ),
        scratch_shapes=[
            pltpu.VMEM((rows + LANE, width + LANE), bf16),
            pltpu.VMEM((group, rows, width + LANE), bf16),
        ],
        compiler_params=params(),
        name="match",
    )(counts, slopes, wide, vert, horiz, images)


def on_device(images, counts, slot_weight, kernel_index, kernel_slope, tap_basis):
    slots, rows, width = images.shape
    parts = lax.axis_size("epoch")
    patches = lax.axis_size("patch")
    chunk = rows // parts
    shifts = (2, 1, 3)
    ahead = accumulate(counts, slot_weight, images, shifts)
    arrived = []
    for i, shift in enumerate(shifts):
        arrived.append(lax.ppermute(ahead[2 * i], "epoch", moves(lambda z, x, y: (z + shift, x, y))))
        arrived.append(lax.ppermute(ahead[2 * i + 1], "epoch", moves(lambda z, x, y: (z, x, y + shift))))
    here = accumulate(counts, slot_weight, images, (0,))
    keep, send = fold((*here, *arrived))
    got = lax.ppermute(send, "epoch", moves(lambda z, x, y: (z, x + 1, y)))
    pieces = list(cut(keep, got))
    for shift in (2, 1, 3):
        ring = moves(lambda z, x, y: (z, x, y + shift) if x == 0 else (z + shift, x, y))
        pieces[shift] = lax.ppermute(pieces[shift], "epoch", ring)
    own, first, last = share(pieces, chunk, width)
    low = lax.ppermute(last, "patch", [(i, i + 1) for i in range(patches - 1)])
    high = lax.ppermute(first, "patch", [(i + 1, i) for i in range(patches - 1)])
    vert, horiz = tap_bands(kernel_index[0], tap_basis)
    copies = widen(own, low, high, parts)
    wide = lax.all_to_all(copies, "epoch", 0, 0, tiled=True)
    differences, template = match(counts, kernel_slope, wide, vert, horiz, images)
    return (template, differences)


def solution(mesh):
    in_specs = (
        P("epoch", None, "patch"),
        P("patch", "epoch"),
        P("patch", "epoch"),
        P("patch", "epoch", None),
        P("patch", "epoch"),
        P(),
    )
    out_specs = (P(None, "patch"), P("epoch", None, "patch"))
    return jax.shard_map(
        on_device, mesh=mesh, in_specs=in_specs, out_specs=out_specs, check_vma=False
    )
```

```python
import functools

import jax
import jax.numpy as jnp
from jax import lax
from jax.experimental import pallas as pl
from jax.experimental.pallas import tpu as pltpu
from jax.sharding import PartitionSpec as P

f32 = jnp.float32
bf16 = jnp.bfloat16
LANE = 128
STEPS = 32767.0
WEIGHT_STEPS = 2.0**17
PAD = 16
VMEM_LIMIT = 44 * 2**20


def smem():
    return pl.BlockSpec(memory_space=pltpu.SMEM)


def vmem():
    return pl.BlockSpec(memory_space=pltpu.VMEM)


def params():
    return pltpu.CompilerParams(vmem_limit_bytes=VMEM_LIMIT)


def bands_kernel(index_ref, basis_ref, vert_ref, horiz_ref, *, slots, taps):
    lead = PAD - taps // 2
    lane = lax.broadcasted_iota(jnp.int32, (8, 2 * LANE), 1)

    def body(s, _):
        first, second, third = index_ref[s, 0], index_ref[s, 1], index_ref[s, 2]
        row0 = jnp.zeros((8, 2 * LANE), f32)
        row1 = jnp.zeros((8, 2 * LANE), f32)
        row2 = jnp.zeros((8, 2 * LANE), f32)
        for t in range(taps):
            row0 = jnp.where(lane == lead + t, basis_ref[first, t], row0)
            back = lane == 2 * LANE - lead - t
            row1 = jnp.where(back, basis_ref[second, t], row1)
            row2 = jnp.where(back, basis_ref[third, t], row2)
        row2 = jnp.concatenate([row2[:, LANE:], row2[:, :LANE]], axis=1)
        for base in range(0, 2 * LANE, 16):
            if base < LANE:
                halves = [pltpu.roll(row0, base + 8 * h, 1, stride=1, stride_axis=0) for h in range(2)]
                vert_ref[s, base : base + 16, :] = jnp.concatenate(halves, axis=0).astype(bf16)
            halves = []
            for h in range(2):
                r1 = pltpu.roll(row1, base + 8 * h, 1, stride=1, stride_axis=0)
                r2 = pltpu.roll(row2, base + 8 * h, 1, stride=1, stride_axis=0)
                halves.append(jnp.concatenate([r1[:, :LANE], r2[:, LANE:]], axis=1))
            horiz_ref[s, base : base + 16, :] = jnp.concatenate(halves, axis=0).astype(bf16)
        return 0

    lax.fori_loop(0, slots, body, 0)


def tap_bands(index, basis):
    slots = index.shape[0]
    return pl.pallas_call(
        functools.partial(bands_kernel, slots=slots, taps=basis.shape[1]),
        out_shape=(
            jax.ShapeDtypeStruct((slots, LANE, 2 * LANE), bf16),
            jax.ShapeDtypeStruct((slots, 2 * LANE, 2 * LANE), bf16),
        ),
        in_specs=[smem(), smem()],
        out_specs=(vmem(), vmem()),
        compiler_params=params(),
        name="tap_bands",
    )(index, basis)


def pack(parts, weight_word, out_ref, base):
    top = jnp.abs(parts[0])
    for part in parts[1:]:
        top = jnp.maximum(top, jnp.abs(part))
    exponent = jnp.ceil(jnp.log2(jnp.maximum(top, 1e-30)) + 0.002)
    factor = STEPS / jnp.exp2(exponent)
    words = [jnp.round(part * factor).astype(jnp.int32) for part in parts]
    half = len(parts) // 2
    for i in range(half):
        out_ref[base + 8 * i : base + 8 * i + 8, :] = (words[half + i] << 16) | (words[i] & 0xFFFF)
    out_ref[base + 8 * half : base + 8 * half + 8, :] = weight_word + (exponent.astype(jnp.int32) + 128)


def accumulate_kernel(count_ref, weight_ref, image_ref, out_ref, held, arrived, *, chunk):
    slots, rows, width = image_ref.shape
    blocks, _, block, _ = held.shape
    copies = [
        pltpu.make_async_copy(image_ref.at[:, n * block : (n + 1) * block, :], held.at[n], arrived.at[n])
        for n in range(blocks)
    ]
    for copy in copies:
        copy.start()
    weights = [jnp.where(s < count_ref[0, 0], weight_ref[0, s], 0.0) for s in range(slots)]
    total = weights[0]
    for s in range(1, slots):
        total = total + weights[s]
    weight_word = jnp.round(jnp.full((8, LANE), total, f32) * WEIGHT_STEPS).astype(jnp.int32) << 8
    cols = width // LANE
    stride = (cols + 1) * 8
    for n, copy in enumerate(copies):
        copy.wait()
        for q in range(block // chunk):
            upper, lower = [], []
            for c in range(cols):
                at = slice(c * LANE, (c + 1) * LANE)
                here = slice(q * chunk, (q + 1) * chunk)
                part = held[n, 0, here, at].astype(f32) * weights[0]
                for s in range(1, slots):
                    part = part + held[n, s, here, at].astype(f32) * weights[s]
                upper.append(part[:8])
                lower.append(part[8:])
            pack(upper + lower, weight_word, out_ref, (n * (block // chunk) + q) * stride)


def accumulate(counts, weight, images, chunk=16, block=64):
    slots, rows, width = images.shape
    return pl.pallas_call(
        functools.partial(accumulate_kernel, chunk=chunk),
        out_shape=jax.ShapeDtypeStruct((rows // chunk * (width // LANE + 1) * 8, LANE), jnp.int32),
        in_specs=[smem(), smem(), pl.BlockSpec(memory_space=pl.ANY)],
        out_specs=vmem(),
        scratch_shapes=[
            pltpu.VMEM((rows // block, slots, block, width), bf16),
            pltpu.SemaphoreType.DMA((rows // block,)),
        ],
        compiler_params=params(),
        name="accumulate",
    )(counts, weight, images)


def share_kernel(piece_ref, own_ref, first_ref, last_ref):
    parts = piece_ref.shape[0]
    cols = own_ref.shape[1] // LANE
    upper, lower, weight = [None] * cols, [None] * cols, None
    for p in range(parts):
        meta = piece_ref[p, 8 * cols :, :]
        weight = meta >> 8 if weight is None else weight + (meta >> 8)
        scale = jnp.exp2(((meta & 0xFF) - 128).astype(f32)) / STEPS
        for c in range(cols):
            word = piece_ref[p, 8 * c : 8 * c + 8, :]
            up = ((word << 16) >> 16).astype(f32) * scale
            low = (word >> 16).astype(f32) * scale
            upper[c] = up if p == 0 else upper[c] + up
            lower[c] = low if p == 0 else lower[c] + low
    weight = weight.astype(f32) / WEIGHT_STEPS
    for c in range(cols):
        block = jnp.concatenate([upper[c] / weight, lower[c] / weight], axis=0).astype(bf16)
        own_ref[:, c * LANE : (c + 1) * LANE] = block
        if c == 0:
            first_ref[...] = block
        if c == cols - 1:
            last_ref[...] = block


def share(pieces, chunk, width):
    return pl.pallas_call(
        share_kernel,
        out_shape=(
            jax.ShapeDtypeStruct((chunk, width), bf16),
            jax.ShapeDtypeStruct((chunk, LANE), bf16),
            jax.ShapeDtypeStruct((chunk, LANE), bf16),
        ),
        in_specs=[vmem()],
        out_specs=(vmem(), vmem(), vmem()),
        compiler_params=params(),
        name="share",
    )(pieces)


def widen_kernel(own_ref, low_ref, high_ref, out_ref, *, parts):
    rows, width = own_ref.shape
    cols = width // LANE
    lane = lax.broadcasted_iota(jnp.int32, (rows, LANE), 1)
    before = pltpu.roll(low_ref[...].astype(f32), PAD, 1)
    for c in range(cols + 1):
        here = own_ref[:, c * LANE : (c + 1) * LANE] if c < cols else high_ref[...]
        here = pltpu.roll(here.astype(f32), PAD, 1)
        block = jnp.where(lane < PAD, before, here).astype(bf16)
        for p in range(parts):
            out_ref[p, :, c * LANE : (c + 1) * LANE] = block
        before = here


def widen(own, low, high, parts):
    rows, width = own.shape
    return pl.pallas_call(
        functools.partial(widen_kernel, parts=parts),
        out_shape=jax.ShapeDtypeStruct((parts, rows, width + LANE), bf16),
        in_specs=[vmem()] * 3,
        out_specs=vmem(),
        compiler_params=params(),
        name="widen",
    )(own, low, high)


def match_kernel(
    count_ref, slope_ref, wide_ref, vert_ref, horiz_ref, image_ref, diff_ref, template_ref, padded, vertical, *, group
):
    step = pl.program_id(0)
    rows, width = image_ref.shape[1:]
    cols = width // LANE
    count = count_ref[0, 0]

    @pl.when(step == 0)
    def _():
        padded[0:PAD, :] = jnp.zeros((PAD, width + LANE), bf16)
        padded[PAD + rows :, :] = jnp.zeros((LANE - PAD, width + LANE), bf16)
        padded[PAD : PAD + rows, :] = wide_ref[...]

    @pl.when(step < rows // LANE)
    def _():
        lane = lax.broadcasted_iota(jnp.int32, (LANE, LANE), 1)
        at = pl.ds(pl.multiple_of(step * LANE, LANE), LANE)
        here = pltpu.roll(wide_ref[at, :LANE].astype(f32), LANE - PAD, 1)
        for c in range(cols):
            after = pltpu.roll(wide_ref[at, (c + 1) * LANE : (c + 2) * LANE].astype(f32), LANE - PAD, 1)
            template_ref[:, c * LANE : (c + 1) * LANE] = jnp.where(lane < LANE - PAD, here, after).astype(bf16)
            here = after

    @pl.when(step * group < count)
    def _():
        band = vert_ref[...].reshape(group * LANE, 2 * LANE)
        for n in range(rows // LANE):
            for j in range(0, cols + 1, 2):
                at = slice(j * LANE, min(j + 2, cols + 1) * LANE)
                part = jnp.dot(band, padded[n * LANE : (n + 2) * LANE, at], preferred_element_type=f32).astype(bf16)
                for g in range(group):
                    vertical[g, n * LANE : (n + 1) * LANE, at] = part[g * LANE : (g + 1) * LANE]
        start = lax.axis_index("patch") * width
        center = width * lax.axis_size("patch") / 2
        column = lax.broadcasted_iota(jnp.int32, (8, LANE), 1) + start
        for g in range(group):
            slot = step * group + g
            live = slot < count
            slope = slope_ref[0, slot]
            for m in range(cols):
                at = slice(m * LANE, (m + 1) * LANE)
                position = ((column + m * LANE).astype(f32) + 0.5 - center) / center
                factor = (slope * position)[0:1]
                both = jnp.dot(vertical[g, :, m * LANE : (m + 2) * LANE], horiz_ref[g], preferred_element_type=f32)
                matched = both[:, :LANE] + factor * both[:, LANE:]
                result = jnp.where(live, image_ref[g, :, at].astype(f32) - matched, 0.0)
                diff_ref[g, :, at] = result.astype(bf16)

    @pl.when(step * group >= count)
    def _():
        diff_ref[...] = jnp.zeros(diff_ref.shape, bf16)


def match(counts, slopes, wide, vert, horiz, images, group=2):
    slots, rows, width = images.shape
    last = rows // LANE - 1
    return pl.pallas_call(
        functools.partial(match_kernel, group=group),
        grid=(slots // group,),
        out_shape=(jax.ShapeDtypeStruct(images.shape, bf16), jax.ShapeDtypeStruct((rows, width), bf16)),
        in_specs=[
            smem(),
            smem(),
            vmem(),
            pl.BlockSpec((group, LANE, 2 * LANE), lambda i: (i, 0, 0)),
            pl.BlockSpec((group, 2 * LANE, 2 * LANE), lambda i: (i, 0, 0)),
            pl.BlockSpec((group, rows, width), lambda i: (i, 0, 0)),
        ],
        out_specs=(
            pl.BlockSpec((group, rows, width), lambda i: (i, 0, 0)),
            pl.BlockSpec((LANE, width), lambda i: (jnp.minimum(i, last), 0)),
        ),
        scratch_shapes=[
            pltpu.VMEM((rows + LANE, width + LANE), bf16),
            pltpu.VMEM((group, rows, width + LANE), bf16),
        ],
        compiler_params=params(),
        name="match",
    )(counts, slopes, wide, vert, horiz, images)


def on_device(images, counts, slot_weight, kernel_index, kernel_slope, tap_basis):
    slots, rows, width = images.shape
    parts = lax.axis_size("epoch")
    patches = lax.axis_size("patch")
    chunk = rows // parts
    partial = accumulate(counts, slot_weight, images, chunk)
    pieces = lax.all_to_all(partial, "epoch", 0, 0, tiled=True)
    own, first, last = share(pieces.reshape(parts, -1, LANE), chunk, width)
    low = lax.ppermute(last, "patch", [(i, i + 1) for i in range(patches - 1)])
    high = lax.ppermute(first, "patch", [(i + 1, i) for i in range(patches - 1)])
    vert, horiz = tap_bands(kernel_index[0], tap_basis)
    copies = widen(own, low, high, parts)
    wide = lax.all_to_all(copies, "epoch", 0, 0, tiled=True).reshape(rows, width + LANE)
    differences, template = match(counts, kernel_slope, wide, vert, horiz, images)
    return (template, differences)


def solution(mesh):
    in_specs = (
        P("epoch", None, "patch"),
        P("patch", "epoch"),
        P("patch", "epoch"),
        P("patch", "epoch", None),
        P("patch", "epoch"),
        P(),
    )
    out_specs = (P(None, "patch"), P("epoch", None, "patch"))
    return jax.shard_map(
        on_device, mesh=mesh, in_specs=in_specs, out_specs=out_specs, check_vma=False
    )
```

```python
import functools

import jax
import jax.numpy as jnp
from jax import lax
from jax.experimental import pallas as pl
from jax.experimental.pallas import tpu as pltpu
from jax.sharding import PartitionSpec as P

f32 = jnp.float32
bf16 = jnp.bfloat16
LANE = 128
STEPS = 32767.0
WEIGHT_STEPS = 2.0**17
PAD = 16
VMEM_LIMIT = 50 * 2**20
GROUP = 2


def smem():
    return pl.BlockSpec(memory_space=pltpu.SMEM)


def vmem():
    return pl.BlockSpec(memory_space=pltpu.VMEM)


def params():
    return pltpu.CompilerParams(vmem_limit_bytes=VMEM_LIMIT)


def bands_kernel(basis_ref, vert_ref, horiz_ref):
    profiles, taps = basis_ref.shape
    lead = PAD - taps // 2
    lane = lax.broadcasted_iota(jnp.int32, (8, 2 * LANE), 1)

    def body(b, _):
        down = jnp.zeros((8, 2 * LANE), f32)
        across = jnp.zeros((8, 2 * LANE), f32)
        for t in range(taps):
            down = jnp.where(lane == lead + t, basis_ref[b, t], down)
            across = jnp.where(lane == 2 * LANE - lead - t, basis_ref[b, t], across)
        for base in range(0, 2 * LANE, 16):
            if base < LANE:
                halves = [pltpu.roll(down, base + 8 * h, 1, stride=1, stride_axis=0) for h in range(2)]
                vert_ref[b, base : base + 16, :] = jnp.concatenate(halves, axis=0).astype(bf16)
            halves = [pltpu.roll(across, base + 8 * h, 1, stride=1, stride_axis=0) for h in range(2)]
            horiz_ref[b, base : base + 16, :] = jnp.concatenate(halves, axis=0)[:, :LANE].astype(bf16)
        return 0

    lax.fori_loop(0, profiles, body, 0)


def tap_bands(basis):
    profiles = basis.shape[0]
    return pl.pallas_call(
        bands_kernel,
        out_shape=(
            jax.ShapeDtypeStruct((profiles, LANE, 2 * LANE), bf16),
            jax.ShapeDtypeStruct((profiles, 2 * LANE, LANE), bf16),
        ),
        in_specs=[smem()],
        out_specs=(vmem(), vmem()),
        compiler_params=params(),
        name="tap_bands",
    )(basis)


def pack(parts, weight_word, out_ref, base):
    top = jnp.abs(parts[0])
    for part in parts[1:]:
        top = jnp.maximum(top, jnp.abs(part))
    exponent = jnp.ceil(jnp.log2(jnp.maximum(top, 1e-30)) + 0.002)
    factor = STEPS / jnp.exp2(exponent)
    words = [jnp.round(part * factor).astype(jnp.int32) for part in parts]
    half = len(parts) // 2
    for i in range(half):
        out_ref[base + 8 * i : base + 8 * i + 8, :] = (words[half + i] << 16) | (words[i] & 0xFFFF)
    out_ref[base + 8 * half : base + 8 * half + 8, :] = weight_word + (exponent.astype(jnp.int32) + 128)


def accumulate_kernel(count_ref, weight_ref, image_ref, out_ref, held, arrived, *, chunk):
    slots, rows, width = image_ref.shape
    blocks, _, block, _ = held.shape
    copies = [
        pltpu.make_async_copy(image_ref.at[:, n * block : (n + 1) * block, :], held.at[n], arrived.at[n])
        for n in range(blocks)
    ]
    for copy in copies:
        copy.start()
    weights = [jnp.where(s < count_ref[0, 0], weight_ref[0, s], 0.0) for s in range(slots)]
    total = weights[0]
    for s in range(1, slots):
        total = total + weights[s]
    weight_word = jnp.round(jnp.full((8, LANE), total, f32) * WEIGHT_STEPS).astype(jnp.int32) << 8
    cols = width // LANE
    stride = (cols + 1) * 8
    for n, copy in enumerate(copies):
        copy.wait()
        for q in range(block // chunk):
            upper, lower = [], []
            for c in range(cols):
                at = slice(c * LANE, (c + 1) * LANE)
                here = slice(q * chunk, (q + 1) * chunk)
                part = held[n, 0, here, at].astype(f32) * weights[0]
                for s in range(1, slots):
                    part = part + held[n, s, here, at].astype(f32) * weights[s]
                upper.append(part[:8])
                lower.append(part[8:])
            pack(upper + lower, weight_word, out_ref, (n * (block // chunk) + q) * stride)


def accumulate(counts, weight, images, chunk=16, block=64):
    slots, rows, width = images.shape
    return pl.pallas_call(
        functools.partial(accumulate_kernel, chunk=chunk),
        out_shape=jax.ShapeDtypeStruct((rows // chunk * (width // LANE + 1) * 8, LANE), jnp.int32),
        in_specs=[smem(), smem(), pl.BlockSpec(memory_space=pl.ANY)],
        out_specs=vmem(),
        scratch_shapes=[
            pltpu.VMEM((rows // block, slots, block, width), bf16),
            pltpu.SemaphoreType.DMA((rows // block,)),
        ],
        compiler_params=params(),
        name="accumulate",
    )(counts, weight, images)


def share_kernel(piece_ref, own_ref, first_ref, last_ref):
    parts = piece_ref.shape[0]
    cols = own_ref.shape[1] // LANE
    upper, lower, weight = [None] * cols, [None] * cols, None
    for p in range(parts):
        meta = piece_ref[p, 8 * cols :, :]
        weight = meta >> 8 if weight is None else weight + (meta >> 8)
        scale = jnp.exp2(((meta & 0xFF) - 128).astype(f32)) / STEPS
        for c in range(cols):
            word = piece_ref[p, 8 * c : 8 * c + 8, :]
            up = ((word << 16) >> 16).astype(f32) * scale
            low = (word >> 16).astype(f32) * scale
            upper[c] = up if p == 0 else upper[c] + up
            lower[c] = low if p == 0 else lower[c] + low
    weight = weight.astype(f32) / WEIGHT_STEPS
    for c in range(cols):
        block = jnp.concatenate([upper[c] / weight, lower[c] / weight], axis=0).astype(bf16)
        own_ref[:, c * LANE : (c + 1) * LANE] = block
        if c == 0:
            first_ref[...] = block
        if c == cols - 1:
            last_ref[...] = block


def share(pieces, chunk, width):
    return pl.pallas_call(
        share_kernel,
        out_shape=(
            jax.ShapeDtypeStruct((chunk, width), bf16),
            jax.ShapeDtypeStruct((chunk, LANE), bf16),
            jax.ShapeDtypeStruct((chunk, LANE), bf16),
        ),
        in_specs=[vmem()],
        out_specs=(vmem(), vmem(), vmem()),
        compiler_params=params(),
        name="share",
    )(pieces)


def widen_kernel(own_ref, low_ref, high_ref, out_ref, *, parts):
    rows, width = own_ref.shape
    cols = width // LANE
    lane = lax.broadcasted_iota(jnp.int32, (rows, LANE), 1)
    patch = lax.axis_index("patch")
    low = low_ref[...].astype(f32) * (patch > 0).astype(f32)
    high = high_ref[...].astype(f32) * (patch < lax.axis_size("patch") - 1).astype(f32)
    before = pltpu.roll(low, PAD, 1)
    for c in range(cols + 1):
        here = own_ref[:, c * LANE : (c + 1) * LANE].astype(f32) if c < cols else high
        here = pltpu.roll(here, PAD, 1)
        block = jnp.where(lane < PAD, before, here).astype(bf16)
        for p in range(parts):
            out_ref[p, :, c * LANE : (c + 1) * LANE] = block
        before = here


def widen(own, low, high, parts):
    rows, width = own.shape
    return pl.pallas_call(
        functools.partial(widen_kernel, parts=parts),
        out_shape=jax.ShapeDtypeStruct((parts, rows, width + LANE), bf16),
        in_specs=[vmem()] * 3,
        out_specs=vmem(),
        compiler_params=params(),
        name="widen",
    )(own, low, high)


def match_kernel(
    count_ref,
    index_ref,
    slope_ref,
    wide_ref,
    vert_ref,
    horiz_ref,
    image_ref,
    template_ref,
    diff_ref,
    padded,
    vertical,
    held,
    arrived,
    sent,
    *,
    group,
):
    slots, rows, width = held.shape
    cols = width // LANE
    count = count_ref[0, 0]

    def fetch(s):
        return pltpu.make_async_copy(image_ref.at[s], held.at[s], arrived.at[s])

    def put(s):
        return pltpu.make_async_copy(held.at[s], diff_ref.at[s], sent.at[s])

    for s in range(slots):
        fetch(s).start()

    padded[0:PAD, :] = jnp.zeros((PAD, width + LANE), bf16)
    padded[PAD + rows :, :] = jnp.zeros((LANE - PAD, width + LANE), bf16)
    padded[PAD : PAD + rows, :] = wide_ref[...]

    profiles = vert_ref.shape[0]
    band = vert_ref[...].reshape(profiles * LANE, 2 * LANE)
    for n in range(rows // LANE):
        for j in range(0, cols + 1, 2):
            at = slice(j * LANE, min(j + 2, cols + 1) * LANE)
            part = jnp.dot(band, padded[n * LANE : (n + 2) * LANE, at], preferred_element_type=f32).astype(bf16)
            for b in range(profiles):
                vertical[b, n * LANE : (n + 1) * LANE, at] = part[b * LANE : (b + 1) * LANE]

    lane = lax.broadcasted_iota(jnp.int32, (LANE, LANE), 1)
    for n in range(rows // LANE):
        at = slice(n * LANE, (n + 1) * LANE)
        here = pltpu.roll(wide_ref[at, :LANE].astype(f32), LANE - PAD, 1)
        for c in range(cols):
            after = pltpu.roll(wide_ref[at, (c + 1) * LANE : (c + 2) * LANE].astype(f32), LANE - PAD, 1)
            template_ref[at, c * LANE : (c + 1) * LANE] = jnp.where(lane < LANE - PAD, here, after).astype(bf16)
            here = after

    start = lax.axis_index("patch") * width
    center = width * lax.axis_size("patch") / 2
    column = lax.broadcasted_iota(jnp.int32, (8, LANE), 1) + start

    def match_group(i, _):
        for g in range(group):
            fetch(i * group + g).wait()

        @pl.when(i * group < count)
        def _():
            for g in range(group):
                slot = i * group + g
                live = slot < count
                slope = slope_ref[0, slot]
                first, second, third = index_ref[slot, 0], index_ref[slot, 1], index_ref[slot, 2]
                bands = jnp.concatenate([horiz_ref[second], horiz_ref[third]], axis=1)
                for m in range(cols):
                    at = slice(m * LANE, (m + 1) * LANE)
                    position = ((column + m * LANE).astype(f32) + 0.5 - center) / center
                    factor = (slope * position)[0:1]
                    both = jnp.dot(vertical[first, :, m * LANE : (m + 2) * LANE], bands, preferred_element_type=f32)
                    matched = both[:, :LANE] + factor * both[:, LANE:]
                    result = jnp.where(live, held[slot, :, at].astype(f32) - matched, 0.0)
                    held[slot, :, at] = result.astype(bf16)

        @pl.when(i * group >= count)
        def _():
            for g in range(group):
                held[i * group + g] = jnp.zeros((rows, width), bf16)

        for g in range(group):
            put(i * group + g).start()
        return 0

    lax.fori_loop(0, slots // group, match_group, 0)
    for s in range(slots):
        put(s).wait()


def match(counts, index, slopes, wide, vert, horiz, images, group=GROUP):
    slots, rows, width = images.shape
    return pl.pallas_call(
        functools.partial(match_kernel, group=group),
        out_shape=(jax.ShapeDtypeStruct((rows, width), bf16), jax.ShapeDtypeStruct(images.shape, bf16)),
        in_specs=[smem()] * 3 + [vmem()] * 3 + [pl.BlockSpec(memory_space=pl.ANY)],
        out_specs=(vmem(), pl.BlockSpec(memory_space=pl.ANY)),
        scratch_shapes=[
            pltpu.VMEM((rows + LANE, width + LANE), bf16),
            pltpu.VMEM((vert.shape[0], rows, width + LANE), bf16),
            pltpu.VMEM(images.shape, bf16),
            pltpu.SemaphoreType.DMA((slots,)),
            pltpu.SemaphoreType.DMA((slots,)),
        ],
        compiler_params=params(),
        name="match",
    )(counts, index, slopes, wide, vert, horiz, images)


def on_device(images, counts, slot_weight, kernel_index, kernel_slope, tap_basis):
    slots, rows, width = images.shape
    parts = lax.axis_size("epoch")
    patches = lax.axis_size("patch")
    chunk = rows // parts
    partial = accumulate(counts, slot_weight, images, chunk)
    pieces = lax.all_to_all(partial, "epoch", 0, 0, tiled=True)
    own, first, last = share(pieces.reshape(parts, -1, LANE), chunk, width)
    ring = [(i, (i + 1) % patches) for i in range(patches)]
    low = lax.ppermute(last, "patch", ring)
    high = lax.ppermute(first, "patch", [(target, source) for source, target in ring])
    vert, horiz = tap_bands(tap_basis)
    copies = widen(own, low, high, parts)
    wide = lax.all_to_all(copies, "epoch", 0, 0, tiled=True).reshape(rows, width + LANE)
    template, differences = match(counts, kernel_index[0], kernel_slope, wide, vert, horiz, images)
    return (template, differences)


def solution(mesh):
    in_specs = (
        P("epoch", None, "patch"),
        P("patch", "epoch"),
        P("patch", "epoch"),
        P("patch", "epoch", None),
        P("patch", "epoch"),
        P(),
    )
    out_specs = (P(None, "patch"), P("epoch", None, "patch"))
    return jax.shard_map(
        on_device, mesh=mesh, in_specs=in_specs, out_specs=out_specs, check_vma=False
    )
```

```python
import functools

import jax
import jax.numpy as jnp
from jax import lax
from jax.experimental import pallas as pl
from jax.experimental.pallas import tpu as pltpu
from jax.sharding import PartitionSpec as P

f32 = jnp.float32
bf16 = jnp.bfloat16
LANE = 128
STEPS = 32767.0
WEIGHT_STEPS = 2.0**17
PAD = 16
GROUP = 2


def smem():
    return pl.BlockSpec(memory_space=pltpu.SMEM)


def vmem():
    return pl.BlockSpec(memory_space=pltpu.VMEM)


def params(limit):
    return pltpu.CompilerParams(vmem_limit_bytes=limit * 2**20)


def bands_kernel(basis_ref, image_ref, vert_ref, horiz_ref, held_ref, arrived):
    fetches = [
        pltpu.make_async_copy(image_ref.at[s], held_ref.at[s], arrived.at[s]) for s in range(image_ref.shape[0])
    ]
    for copy in fetches:
        copy.start()
    profiles, taps = basis_ref.shape
    lead = PAD - taps // 2
    lane = lax.broadcasted_iota(jnp.int32, (8, 2 * LANE), 1)

    def body(b, _):
        down = jnp.zeros((8, 2 * LANE), f32)
        across = jnp.zeros((8, 2 * LANE), f32)
        for t in range(taps):
            down = jnp.where(lane == lead + t, basis_ref[b, t], down)
            across = jnp.where(lane == 2 * LANE - lead - t, basis_ref[b, t], across)
        for base in range(0, 2 * LANE, 16):
            if base < LANE:
                halves = [pltpu.roll(down, base + 8 * h, 1, stride=1, stride_axis=0) for h in range(2)]
                vert_ref[b, base : base + 16, :] = jnp.concatenate(halves, axis=0).astype(bf16)
            halves = [pltpu.roll(across, base + 8 * h, 1, stride=1, stride_axis=0) for h in range(2)]
            horiz_ref[b, base : base + 16, :] = jnp.concatenate(halves, axis=0)[:, :LANE].astype(bf16)
        return 0

    lax.fori_loop(0, profiles, body, 0)
    for copy in fetches:
        copy.wait()


def tap_bands(basis, images):
    profiles = basis.shape[0]
    return pl.pallas_call(
        bands_kernel,
        out_shape=(
            jax.ShapeDtypeStruct((profiles, LANE, 2 * LANE), bf16),
            jax.ShapeDtypeStruct((profiles, 2 * LANE, LANE), bf16),
            jax.ShapeDtypeStruct(images.shape, bf16),
        ),
        in_specs=[smem(), pl.BlockSpec(memory_space=pl.ANY)],
        out_specs=(vmem(), vmem(), vmem()),
        scratch_shapes=[pltpu.SemaphoreType.DMA((images.shape[0],))],
        compiler_params=params(38),
        name="tap_bands",
    )(basis, images)


def pack(parts, weight_word, out_ref, base):
    top = jnp.abs(parts[0])
    for part in parts[1:]:
        top = jnp.maximum(top, jnp.abs(part))
    exponent = jnp.ceil(jnp.log2(jnp.maximum(top, 1e-30)) + 0.002)
    factor = STEPS / jnp.exp2(exponent)
    words = [jnp.round(part * factor).astype(jnp.int32) for part in parts]
    half = len(parts) // 2
    for i in range(half):
        out_ref[base + 8 * i : base + 8 * i + 8, :] = (words[half + i] << 16) | (words[i] & 0xFFFF)
    out_ref[base + 8 * half : base + 8 * half + 8, :] = weight_word + (exponent.astype(jnp.int32) + 128)


def accumulate_kernel(counts_ref, weights_ref, image_ref, out_ref, held, arrived, count_ref, weight_ref, placed, *, chunk):
    slots, rows, width = image_ref.shape
    blocks, _, block, _ = held.shape
    copies = [
        pltpu.make_async_copy(image_ref.at[:, n * block : (n + 1) * block, :], held.at[n], arrived.at[n])
        for n in range(blocks)
    ]
    small = (
        pltpu.make_async_copy(counts_ref, count_ref, placed.at[0]),
        pltpu.make_async_copy(weights_ref, weight_ref, placed.at[1]),
    )
    for copy in (*small, *copies):
        copy.start()
    for copy in small:
        copy.wait()
    weights = [jnp.where(s < count_ref[0, 0], weight_ref[0, s], 0.0) for s in range(slots)]
    total = weights[0]
    for s in range(1, slots):
        total = total + weights[s]
    weight_word = jnp.round(jnp.full((8, LANE), total, f32) * WEIGHT_STEPS).astype(jnp.int32) << 8
    cols = width // LANE
    stride = (cols + 1) * 8
    for n, copy in enumerate(copies):
        copy.wait()
        for q in range(block // chunk):
            upper, lower = [], []
            for c in range(cols):
                at = slice(c * LANE, (c + 1) * LANE)
                here = slice(q * chunk, (q + 1) * chunk)
                part = held[n, 0, here, at].astype(f32) * weights[0]
                for s in range(1, slots):
                    part = part + held[n, s, here, at].astype(f32) * weights[s]
                upper.append(part[:8])
                lower.append(part[8:])
            pack(upper + lower, weight_word, out_ref, (n * (block // chunk) + q) * stride)


def accumulate(counts, weight, images, chunk=16, block=64):
    slots, rows, width = images.shape
    return pl.pallas_call(
        functools.partial(accumulate_kernel, chunk=chunk),
        out_shape=jax.ShapeDtypeStruct((rows // chunk * (width // LANE + 1) * 8, LANE), jnp.int32),
        in_specs=[pl.BlockSpec(memory_space=pl.ANY)] * 3,
        out_specs=vmem(),
        scratch_shapes=[
            pltpu.VMEM((rows // block, slots, block, width), bf16),
            pltpu.SemaphoreType.DMA((rows // block,)),
            pltpu.SMEM(counts.shape, jnp.int32),
            pltpu.SMEM(weight.shape, f32),
            pltpu.SemaphoreType.DMA((2,)),
        ],
        compiler_params=params(50),
        name="accumulate",
    )(counts, weight, images)


def share_kernel(piece_ref, out_ref):
    parts, chunk, width = out_ref.shape
    cols = width // LANE
    upper, lower, weight = [None] * cols, [None] * cols, None
    for p in range(parts):
        meta = piece_ref[p, 8 * cols :, :]
        weight = meta >> 8 if weight is None else weight + (meta >> 8)
        scale = jnp.exp2(((meta & 0xFF) - 128).astype(f32)) / STEPS
        for c in range(cols):
            word = piece_ref[p, 8 * c : 8 * c + 8, :]
            up = ((word << 16) >> 16).astype(f32) * scale
            low = (word >> 16).astype(f32) * scale
            upper[c] = up if p == 0 else upper[c] + up
            lower[c] = low if p == 0 else lower[c] + low
    weight = weight.astype(f32) / WEIGHT_STEPS
    lane = lax.broadcasted_iota(jnp.int32, (chunk, LANE), 1)
    turned = [
        pltpu.roll(jnp.concatenate([upper[c] / weight, lower[c] / weight], axis=0), PAD, 1) for c in range(cols)
    ]
    for c in range(cols):
        block = jnp.where(lane < PAD, turned[c - 1], turned[c]).astype(bf16)
        for p in range(parts):
            out_ref[p, :, c * LANE : (c + 1) * LANE] = block


def share(pieces, chunk, width):
    parts = pieces.shape[0]
    return pl.pallas_call(
        share_kernel,
        out_shape=jax.ShapeDtypeStruct((parts, chunk, width), bf16),
        in_specs=[vmem()],
        out_specs=vmem(),
        compiler_params=params(16),
        name="share",
    )(pieces)


def vertical_step(vert_ref, padded, store):
    profiles = vert_ref.shape[0]
    rows, width = padded.shape[0] - LANE, padded.shape[1]
    band = vert_ref[...].reshape(profiles * LANE, 2 * LANE)
    for n in range(rows // LANE):
        for j in range(0, width, 2 * LANE):
            at = slice(j, min(j + 2 * LANE, width))
            part = jnp.dot(band, padded[n * LANE : (n + 2) * LANE, at], preferred_element_type=f32).astype(bf16)
            for b in range(profiles):
                store(b, slice(n * LANE, (n + 1) * LANE), at, part[b * LANE : (b + 1) * LANE])


def pack_ends_kernel(turned_ref, out_ref):
    part = out_ref.shape[0]
    lane = lax.broadcasted_iota(jnp.int32, out_ref.shape, 1)
    ends = turned_ref[:part, :LANE].astype(f32)
    for n in range(1, turned_ref.shape[0] // part):
        here = pltpu.roll(turned_ref[n * part : (n + 1) * part, :LANE].astype(f32), 2 * PAD * n, 1)
        ends = jnp.where(lane < 2 * PAD * n, ends, here)
    out_ref[...] = ends.astype(bf16)


def pack_ends(turned):
    return pl.pallas_call(
        pack_ends_kernel,
        out_shape=jax.ShapeDtypeStruct((turned.shape[0] * 2 * PAD // LANE, LANE), bf16),
        grid=(1,),
        in_specs=[pl.BlockSpec((turned.shape[0], LANE), lambda i: (0, 0))],
        out_specs=pl.BlockSpec((turned.shape[0] * 2 * PAD // LANE, LANE), lambda i: (0, 0)),
        compiler_params=params(16),
        name="pack_ends",
    )(turned)


def inner_kernel(turned_ref, vert_ref, template_ref, vertical_ref, padded, template, written):
    rows, width = turned_ref.shape
    cols = width // LANE
    padded[0:PAD, :] = jnp.zeros((PAD, width - LANE), bf16)
    padded[PAD + rows :, :] = jnp.zeros((LANE - PAD, width - LANE), bf16)
    padded[PAD : PAD + rows, :] = turned_ref[:, LANE:]

    lane = lax.broadcasted_iota(jnp.int32, (LANE, LANE), 1)
    for n in range(rows // LANE):
        at = slice(n * LANE, (n + 1) * LANE)
        back = [
            pltpu.roll(turned_ref[at, c * LANE : (c + 1) * LANE].astype(f32), LANE - PAD, 1) for c in range(cols)
        ]
        for c in range(cols):
            block = jnp.where(lane < LANE - PAD, back[c], back[(c + 1) % cols])
            template[at, c * LANE : (c + 1) * LANE] = block.astype(bf16)
    copy = pltpu.make_async_copy(template, template_ref, written)
    copy.start()

    def store(b, at, to, part):
        vertical_ref[b, at, to] = part

    @pl.loop(0, 1)
    def _(_):
        vertical_step(vert_ref, padded, store)

    copy.wait()


def match_inner(turned, vert):
    rows, width = turned.shape
    hbm = pl.BlockSpec(memory_space=pl.ANY)
    return pl.pallas_call(
        inner_kernel,
        out_shape=(
            jax.ShapeDtypeStruct((rows, width), bf16),
            jax.ShapeDtypeStruct((vert.shape[0], rows, width - LANE), bf16),
        ),
        in_specs=[vmem(), vmem()],
        out_specs=(hbm, vmem()),
        scratch_shapes=[
            pltpu.VMEM((rows + LANE, width - LANE), bf16),
            pltpu.VMEM((rows, width), bf16),
            pltpu.SemaphoreType.DMA,
        ],
        cost_estimate=pl.CostEstimate(flops=10**10, bytes_accessed=10**7, transcendentals=0),
        compiler_params=params(16),
        name="match_inner",
    )(turned, vert)


def match_kernel(
    count_ref,
    index_ref,
    slope_ref,
    turned_ref,
    low_ref,
    high_ref,
    vert_ref,
    horiz_ref,
    inner_ref,
    image_ref,
    diff_ref,
    padded,
    outer,
    staged,
    sent,
    *,
    group,
):
    slots, rows, width = staged.shape
    cols = width // LANE
    count = count_ref[0, 0]
    patch = lax.axis_index("patch")

    def put(s):
        return pltpu.make_async_copy(staged.at[s], diff_ref.at[s], sent.at[s])

    @pl.when(count > 0)
    def _():
        padded[0:PAD, :] = jnp.zeros((PAD, 2 * LANE), bf16)
        padded[PAD + rows :, :] = jnp.zeros((LANE - PAD, 2 * LANE), bf16)
        part = low_ref.shape[0]
        lane = lax.broadcasted_iota(jnp.int32, (part, LANE), 1)
        low = low_ref[...].astype(f32) * (patch > 0).astype(f32)
        high = high_ref[...].astype(f32) * (patch < lax.axis_size("patch") - 1).astype(f32)
        for n in range(rows // part):
            own = turned_ref[n * part : (n + 1) * part, :LANE].astype(f32)
            left = pltpu.roll(low, LANE - 2 * PAD * n, 1) if n else low
            right = pltpu.roll(high, LANE - 2 * PAD * n, 1) if n else high
            at = slice(PAD + n * part, PAD + (n + 1) * part)
            padded[at, :LANE] = jnp.where(lane < PAD, left, own).astype(bf16)
            padded[at, LANE:] = jnp.where(lane < PAD, own, right).astype(bf16)

        def store(b, at, _, part):
            outer[b, at, :LANE] = part[:, :LANE]
            outer[b, at, 3 * LANE :] = part[:, LANE:]

        vertical_step(vert_ref, padded, store)
        for b in range(vert_ref.shape[0]):
            outer[b, :, LANE : 2 * LANE] = inner_ref[b, :, :LANE]
            outer[b, :, 2 * LANE : 3 * LANE] = inner_ref[b, :, width - 2 * LANE :]

    center = width * lax.axis_size("patch") / 2
    column = lax.broadcasted_iota(jnp.int32, (8, LANE), 1) + patch * width

    def match_group(i, _):
        @pl.when(i * group < count)
        def _():
            for g in range(group):
                slot = i * group + g
                live = slot < count
                slope = slope_ref[0, slot]
                first, second, third = index_ref[slot, 0], index_ref[slot, 1], index_ref[slot, 2]
                bands = jnp.concatenate([horiz_ref[second], horiz_ref[third]], axis=1)
                for m in range(cols):
                    at = slice(m * LANE, (m + 1) * LANE)
                    if m == 0:
                        window = outer[first, :, : 2 * LANE]
                    elif m == cols - 1:
                        window = outer[first, :, 2 * LANE :]
                    else:
                        window = inner_ref[first, :, (m - 1) * LANE : (m + 1) * LANE]
                    position = ((column + m * LANE).astype(f32) + 0.5 - center) / center
                    factor = (slope * position)[0:1]
                    both = jnp.dot(window, bands, preferred_element_type=f32)
                    matched = both[:, :LANE] + factor * both[:, LANE:]
                    result = jnp.where(live, image_ref[slot, :, at].astype(f32) - matched, 0.0)
                    staged[slot, :, at] = result.astype(bf16)
                put(slot).start()

        @pl.when(i * group >= count)
        def _():
            for g in range(group):
                staged[i * group + g] = jnp.zeros((rows, width), bf16)
                put(i * group + g).start()

        return 0

    lax.fori_loop(0, slots // group, match_group, 0)
    for s in range(slots):
        put(s).wait()


def match(counts, index, slopes, turned, low, high, vert, horiz, inner, images, group=GROUP):
    slots, rows, width = images.shape
    return pl.pallas_call(
        functools.partial(match_kernel, group=group),
        out_shape=jax.ShapeDtypeStruct(images.shape, bf16),
        in_specs=[smem()] * 3 + [vmem()] * 7,
        out_specs=pl.BlockSpec(memory_space=pl.ANY),
        scratch_shapes=[
            pltpu.VMEM((rows + LANE, 2 * LANE), bf16),
            pltpu.VMEM((vert.shape[0], rows, 4 * LANE), bf16),
            pltpu.VMEM(images.shape, bf16),
            pltpu.SemaphoreType.DMA((slots,)),
        ],
        compiler_params=params(24),
        name="match",
    )(counts, index, slopes, turned, low, high, vert, horiz, inner, images)


def on_device(images, counts, slot_weight, kernel_index, kernel_slope, tap_basis):
    slots, rows, width = images.shape
    parts = lax.axis_size("epoch")
    patches = lax.axis_size("patch")
    chunk = rows // parts
    partial = accumulate(counts, slot_weight, images, chunk)
    pieces = lax.all_to_all(partial, "epoch", 0, 0, tiled=True)
    copies = share(pieces.reshape(parts, -1, LANE), chunk, width)
    turned = lax.all_to_all(copies, "epoch", 0, 0, tiled=True).reshape(rows, width)
    vert, horiz, held = tap_bands(tap_basis, images)
    ring = [(i, (i + 1) % patches) for i in range(patches)]
    ends = pack_ends(turned)
    low = lax.ppermute(ends, "patch", ring)
    high = lax.ppermute(ends, "patch", [(target, source) for source, target in ring])
    template, inner = match_inner(turned, vert)
    differences = match(
        counts, kernel_index[0], kernel_slope, turned, low, high, vert, horiz, inner, held
    )
    return (template, differences)


def solution(mesh):
    in_specs = (
        P("epoch", None, "patch"),
        P("patch", "epoch"),
        P("patch", "epoch"),
        P("patch", "epoch", None),
        P("patch", "epoch"),
        P(),
    )
    out_specs = (P(None, "patch"), P("epoch", None, "patch"))
    return jax.shard_map(
        on_device, mesh=mesh, in_specs=in_specs, out_specs=out_specs, check_vma=False
    )
```

```python
import functools

import jax
import jax.numpy as jnp
from jax import lax
from jax.experimental import pallas as pl
from jax.experimental.pallas import tpu as pltpu
from jax.sharding import PartitionSpec as P

f32 = jnp.float32
bf16 = jnp.bfloat16
LANE = 128
STEPS = 32767.0
WEIGHT_STEPS = 2.0**17
PAD = 16
GROUP = 2


def smem():
    return pl.BlockSpec(memory_space=pltpu.SMEM)


def vmem():
    return pl.BlockSpec(memory_space=pltpu.VMEM)


def params(limit):
    return pltpu.CompilerParams(vmem_limit_bytes=limit * 2**20)


def bands_kernel(basis_ref, image_ref, vert_ref, horiz_ref, held_ref, arrived):
    fetches = [
        pltpu.make_async_copy(image_ref.at[s], held_ref.at[s], arrived.at[s]) for s in range(image_ref.shape[0])
    ]
    for copy in fetches:
        copy.start()
    profiles, taps = basis_ref.shape
    lead = PAD - taps // 2
    lane = lax.broadcasted_iota(jnp.int32, (8, 2 * LANE), 1)

    def body(b, _):
        down = jnp.zeros((8, 2 * LANE), f32)
        across = jnp.zeros((8, 2 * LANE), f32)
        for t in range(taps):
            down = jnp.where(lane == lead + t, basis_ref[b, t], down)
            across = jnp.where(lane == 2 * LANE - lead - t, basis_ref[b, t], across)
        for base in range(0, 2 * LANE, 16):
            if base < LANE:
                halves = [pltpu.roll(down, base + 8 * h, 1, stride=1, stride_axis=0) for h in range(2)]
                vert_ref[b, base : base + 16, :] = jnp.concatenate(halves, axis=0).astype(bf16)
            halves = [pltpu.roll(across, base + 8 * h, 1, stride=1, stride_axis=0) for h in range(2)]
            horiz_ref[b, base : base + 16, :] = jnp.concatenate(halves, axis=0)[:, :LANE].astype(bf16)
        return 0

    lax.fori_loop(0, profiles, body, 0)
    for copy in fetches:
        copy.wait()


def tap_bands(basis, images):
    profiles = basis.shape[0]
    return pl.pallas_call(
        bands_kernel,
        out_shape=(
            jax.ShapeDtypeStruct((profiles, LANE, 2 * LANE), bf16),
            jax.ShapeDtypeStruct((profiles, 2 * LANE, LANE), bf16),
            jax.ShapeDtypeStruct(images.shape, bf16),
        ),
        in_specs=[smem(), pl.BlockSpec(memory_space=pl.ANY)],
        out_specs=(vmem(), vmem(), vmem()),
        scratch_shapes=[pltpu.SemaphoreType.DMA((images.shape[0],))],
        compiler_params=params(38),
        name="tap_bands",
    )(basis, images)


def pack(parts, weight_word, out_ref, base):
    top = jnp.abs(parts[0])
    for part in parts[1:]:
        top = jnp.maximum(top, jnp.abs(part))
    exponent = jnp.ceil(jnp.log2(jnp.maximum(top, 1e-30)) + 0.002)
    factor = STEPS / jnp.exp2(exponent)
    words = [jnp.round(part * factor).astype(jnp.int32) for part in parts]
    half = len(parts) // 2
    for i in range(half):
        out_ref[base + 8 * i : base + 8 * i + 8, :] = (words[half + i] << 16) | (words[i] & 0xFFFF)
    out_ref[base + 8 * half : base + 8 * half + 8, :] = weight_word + (exponent.astype(jnp.int32) + 128)


def accumulate_kernel(counts_ref, weights_ref, image_ref, out_ref, held, arrived, count_ref, weight_ref, placed, *, chunk):
    slots, rows, width = image_ref.shape
    blocks, _, block, _ = held.shape
    copies = [
        pltpu.make_async_copy(image_ref.at[:, n * block : (n + 1) * block, :], held.at[n], arrived.at[n])
        for n in range(blocks)
    ]
    small = (
        pltpu.make_async_copy(counts_ref, count_ref, placed.at[0]),
        pltpu.make_async_copy(weights_ref, weight_ref, placed.at[1]),
    )
    for copy in (*small, *copies):
        copy.start()
    for copy in small:
        copy.wait()
    weights = [jnp.where(s < count_ref[0, 0], weight_ref[0, s], 0.0) for s in range(slots)]
    total = weights[0]
    for s in range(1, slots):
        total = total + weights[s]
    weight_word = jnp.round(jnp.full((8, LANE), total, f32) * WEIGHT_STEPS).astype(jnp.int32) << 8
    cols = width // LANE
    stride = (cols + 1) * 8
    for n, copy in enumerate(copies):
        copy.wait()
        for q in range(block // chunk):
            upper, lower = [], []
            for c in range(cols):
                at = slice(c * LANE, (c + 1) * LANE)
                here = slice(q * chunk, (q + 1) * chunk)
                part = held[n, 0, here, at].astype(f32) * weights[0]
                for s in range(1, slots):
                    part = part + held[n, s, here, at].astype(f32) * weights[s]
                upper.append(part[:8])
                lower.append(part[8:])
            pack(upper + lower, weight_word, out_ref, (n * (block // chunk) + q) * stride)


def accumulate(counts, weight, images, chunk=16, block=64):
    slots, rows, width = images.shape
    return pl.pallas_call(
        functools.partial(accumulate_kernel, chunk=chunk),
        out_shape=jax.ShapeDtypeStruct((rows // chunk * (width // LANE + 1) * 8, LANE), jnp.int32),
        in_specs=[pl.BlockSpec(memory_space=pl.ANY)] * 3,
        out_specs=vmem(),
        scratch_shapes=[
            pltpu.VMEM((rows // block, slots, block, width), bf16),
            pltpu.SemaphoreType.DMA((rows // block,)),
            pltpu.SMEM(counts.shape, jnp.int32),
            pltpu.SMEM(weight.shape, f32),
            pltpu.SemaphoreType.DMA((2,)),
        ],
        compiler_params=params(50),
        name="accumulate",
    )(counts, weight, images)


def share_kernel(piece_ref, out_ref):
    parts, chunk, width = out_ref.shape
    cols = width // LANE
    upper, lower, weight = [None] * cols, [None] * cols, None
    for p in range(parts):
        meta = piece_ref[p, 8 * cols :, :]
        weight = meta >> 8 if weight is None else weight + (meta >> 8)
        scale = jnp.exp2(((meta & 0xFF) - 128).astype(f32)) / STEPS
        for c in range(cols):
            word = piece_ref[p, 8 * c : 8 * c + 8, :]
            up = ((word << 16) >> 16).astype(f32) * scale
            low = (word >> 16).astype(f32) * scale
            upper[c] = up if p == 0 else upper[c] + up
            lower[c] = low if p == 0 else lower[c] + low
    weight = weight.astype(f32) / WEIGHT_STEPS
    lane = lax.broadcasted_iota(jnp.int32, (chunk, LANE), 1)
    turned = [
        pltpu.roll(jnp.concatenate([upper[c] / weight, lower[c] / weight], axis=0), PAD, 1) for c in range(cols)
    ]
    for c in range(cols):
        block = jnp.where(lane < PAD, turned[c - 1], turned[c]).astype(bf16)
        for p in range(parts):
            out_ref[p, :, c * LANE : (c + 1) * LANE] = block


def share(pieces, chunk, width):
    parts = pieces.shape[0]
    return pl.pallas_call(
        share_kernel,
        out_shape=jax.ShapeDtypeStruct((parts, chunk, width), bf16),
        in_specs=[vmem()],
        out_specs=vmem(),
        compiler_params=params(16),
        name="share",
    )(pieces)


def vertical_step(vert_ref, padded, store):
    profiles = vert_ref.shape[0]
    rows, width = padded.shape[0] - LANE, padded.shape[1]
    band = vert_ref[...].reshape(profiles * LANE, 2 * LANE)
    for n in range(rows // LANE):
        for j in range(0, width, 2 * LANE):
            at = slice(j, min(j + 2 * LANE, width))
            part = jnp.dot(band, padded[n * LANE : (n + 2) * LANE, at], preferred_element_type=f32).astype(bf16)
            for b in range(profiles):
                store(b, slice(n * LANE, (n + 1) * LANE), at, part[b * LANE : (b + 1) * LANE])


def pack_ends_kernel(turned_ref, out_ref):
    part = out_ref.shape[0]
    lane = lax.broadcasted_iota(jnp.int32, out_ref.shape, 1)
    ends = turned_ref[:part, :LANE].astype(f32)
    for n in range(1, turned_ref.shape[0] // part):
        here = pltpu.roll(turned_ref[n * part : (n + 1) * part, :LANE].astype(f32), 2 * PAD * n, 1)
        ends = jnp.where(lane < 2 * PAD * n, ends, here)
    out_ref[...] = ends.astype(bf16)


def pack_ends(turned):
    return pl.pallas_call(
        pack_ends_kernel,
        out_shape=jax.ShapeDtypeStruct((turned.shape[0] * 2 * PAD // LANE, LANE), bf16),
        grid=(1,),
        in_specs=[pl.BlockSpec((turned.shape[0], LANE), lambda i: (0, 0))],
        out_specs=pl.BlockSpec((turned.shape[0] * 2 * PAD // LANE, LANE), lambda i: (0, 0)),
        compiler_params=params(16),
        name="pack_ends",
    )(turned)


def inner_kernel(turned_ref, vert_ref, vertical_ref, padded):
    rows, width = turned_ref.shape
    padded[0:PAD, :] = jnp.zeros((PAD, width - LANE), bf16)
    padded[PAD + rows :, :] = jnp.zeros((LANE - PAD, width - LANE), bf16)
    padded[PAD : PAD + rows, :] = turned_ref[:, LANE:]

    def store(b, at, to, part):
        vertical_ref[b, at, to] = part

    vertical_step(vert_ref, padded, store)


def match_inner(turned, vert):
    rows, width = turned.shape
    return pl.pallas_call(
        inner_kernel,
        out_shape=jax.ShapeDtypeStruct((vert.shape[0], rows, width - LANE), bf16),
        in_specs=[vmem(), vmem()],
        out_specs=vmem(),
        scratch_shapes=[pltpu.VMEM((rows + LANE, width - LANE), bf16)],
        cost_estimate=pl.CostEstimate(flops=10**10, bytes_accessed=10**7, transcendentals=0),
        compiler_params=params(16),
        name="match_inner",
    )(turned, vert)


def template_kernel(turned_ref, out_ref, done_ref, template_ref, written):
    rows, width = turned_ref.shape
    cols = width // LANE
    lane = lax.broadcasted_iota(jnp.int32, (LANE, LANE), 1)
    for n in range(rows // LANE):
        at = slice(n * LANE, (n + 1) * LANE)
        back = [
            pltpu.roll(turned_ref[at, c * LANE : (c + 1) * LANE].astype(f32), LANE - PAD, 1) for c in range(cols)
        ]
        for c in range(cols):
            block = jnp.where(lane < LANE - PAD, back[c], back[(c + 1) % cols])
            template_ref[at, c * LANE : (c + 1) * LANE] = block.astype(bf16)
    copy = pltpu.make_async_copy(template_ref, out_ref, written)
    copy.start()
    done_ref[...] = jnp.zeros(done_ref.shape, f32)
    copy.wait()


def turn_back(turned):
    return pl.pallas_call(
        template_kernel,
        out_shape=(jax.ShapeDtypeStruct(turned.shape, bf16), jax.ShapeDtypeStruct((8, LANE), f32)),
        in_specs=[vmem()],
        out_specs=(pl.BlockSpec(memory_space=pl.ANY), vmem()),
        scratch_shapes=[pltpu.VMEM(turned.shape, bf16), pltpu.SemaphoreType.DMA],
        cost_estimate=pl.CostEstimate(flops=10**7, bytes_accessed=4 * 10**6, transcendentals=0),
        compiler_params=params(16),
        name="template",
    )(turned)


def match_kernel(
    count_ref,
    index_ref,
    slope_ref,
    turned_ref,
    low_ref,
    high_ref,
    vert_ref,
    horiz_ref,
    inner_ref,
    image_ref,
    _,
    diff_ref,
    padded,
    outer,
    staged,
    sent,
    *,
    group,
):
    slots, rows, width = staged.shape
    cols = width // LANE
    count = count_ref[0, 0]
    patch = lax.axis_index("patch")

    def put(s):
        return pltpu.make_async_copy(staged.at[s], diff_ref.at[s], sent.at[s])

    @pl.when(count > 0)
    def _():
        padded[0:PAD, :] = jnp.zeros((PAD, 2 * LANE), bf16)
        padded[PAD + rows :, :] = jnp.zeros((LANE - PAD, 2 * LANE), bf16)
        part = low_ref.shape[0]
        lane = lax.broadcasted_iota(jnp.int32, (part, LANE), 1)
        low = low_ref[...].astype(f32) * (patch > 0).astype(f32)
        high = high_ref[...].astype(f32) * (patch < lax.axis_size("patch") - 1).astype(f32)
        for n in range(rows // part):
            own = turned_ref[n * part : (n + 1) * part, :LANE].astype(f32)
            left = pltpu.roll(low, LANE - 2 * PAD * n, 1) if n else low
            right = pltpu.roll(high, LANE - 2 * PAD * n, 1) if n else high
            at = slice(PAD + n * part, PAD + (n + 1) * part)
            padded[at, :LANE] = jnp.where(lane < PAD, left, own).astype(bf16)
            padded[at, LANE:] = jnp.where(lane < PAD, own, right).astype(bf16)

        def store(b, at, _, part):
            outer[b, at, :LANE] = part[:, :LANE]
            outer[b, at, 3 * LANE :] = part[:, LANE:]

        vertical_step(vert_ref, padded, store)
        for b in range(vert_ref.shape[0]):
            outer[b, :, LANE : 2 * LANE] = inner_ref[b, :, :LANE]
            outer[b, :, 2 * LANE : 3 * LANE] = inner_ref[b, :, width - 2 * LANE :]

    center = width * lax.axis_size("patch") / 2
    column = lax.broadcasted_iota(jnp.int32, (8, LANE), 1) + patch * width

    def match_group(i, _):
        @pl.when(i * group < count)
        def _():
            for g in range(group):
                slot = i * group + g
                live = slot < count
                slope = slope_ref[0, slot]
                first, second, third = index_ref[slot, 0], index_ref[slot, 1], index_ref[slot, 2]
                bands = jnp.concatenate([horiz_ref[second], horiz_ref[third]], axis=1)
                for m in range(cols):
                    at = slice(m * LANE, (m + 1) * LANE)
                    if m == 0:
                        window = outer[first, :, : 2 * LANE]
                    elif m == cols - 1:
                        window = outer[first, :, 2 * LANE :]
                    else:
                        window = inner_ref[first, :, (m - 1) * LANE : (m + 1) * LANE]
                    position = ((column + m * LANE).astype(f32) + 0.5 - center) / center
                    factor = (slope * position)[0:1]
                    both = jnp.dot(window, bands, preferred_element_type=f32)
                    matched = both[:, :LANE] + factor * both[:, LANE:]
                    result = jnp.where(live, image_ref[slot, :, at].astype(f32) - matched, 0.0)
                    staged[slot, :, at] = result.astype(bf16)
                put(slot).start()

        @pl.when(i * group >= count)
        def _():
            for g in range(group):
                staged[i * group + g] = jnp.zeros((rows, width), bf16)
                put(i * group + g).start()

        return 0

    lax.fori_loop(0, slots // group, match_group, 0)
    for s in range(slots):
        put(s).wait()


def match(counts, index, slopes, turned, low, high, vert, horiz, inner, images, ahead, group=GROUP):
    slots, rows, width = images.shape
    return pl.pallas_call(
        functools.partial(match_kernel, group=group),
        out_shape=jax.ShapeDtypeStruct(images.shape, bf16),
        in_specs=[smem()] * 3 + [vmem()] * 7 + [pl.BlockSpec(memory_space=pl.ANY)],
        out_specs=pl.BlockSpec(memory_space=pl.ANY),
        scratch_shapes=[
            pltpu.VMEM((rows + LANE, 2 * LANE), bf16),
            pltpu.VMEM((vert.shape[0], rows, 4 * LANE), bf16),
            pltpu.VMEM(images.shape, bf16),
            pltpu.SemaphoreType.DMA((slots,)),
        ],
        compiler_params=params(24),
        name="match",
    )(counts, index, slopes, turned, low, high, vert, horiz, inner, images, ahead)


def on_device(images, counts, slot_weight, kernel_index, kernel_slope, tap_basis):
    slots, rows, width = images.shape
    parts = lax.axis_size("epoch")
    patches = lax.axis_size("patch")
    chunk = rows // parts
    partial = accumulate(counts, slot_weight, images, chunk)
    pieces = lax.all_to_all(partial, "epoch", 0, 0, tiled=True)
    copies = share(pieces.reshape(parts, -1, LANE), chunk, width)
    turned = lax.all_to_all(copies, "epoch", 0, 0, tiled=True).reshape(rows, width)
    vert, horiz, held = tap_bands(tap_basis, images)
    ring = [(i, (i + 1) % patches) for i in range(patches)]
    ends = pack_ends(turned)
    high = lax.ppermute(ends, "patch", [(target, source) for source, target in ring])
    low = lax.ppermute(ends, "patch", ring)
    inner = match_inner(turned, vert)
    template, done = turn_back(turned)
    differences = match(
        counts, kernel_index[0], kernel_slope, turned, low, high, vert, horiz, inner, held, done
    )
    return (template, differences)


def solution(mesh):
    in_specs = (
        P("epoch", None, "patch"),
        P("patch", "epoch"),
        P("patch", "epoch"),
        P("patch", "epoch", None),
        P("patch", "epoch"),
        P(),
    )
    out_specs = (P(None, "patch"), P("epoch", None, "patch"))
    return jax.shard_map(
        on_device, mesh=mesh, in_specs=in_specs, out_specs=out_specs, check_vma=False
    )
```

```python
import functools

import jax
import jax.numpy as jnp
from jax import lax
from jax.experimental import pallas as pl
from jax.experimental.pallas import tpu as pltpu
from jax.sharding import PartitionSpec as P

f32 = jnp.float32
bf16 = jnp.bfloat16
LANE = 128
STEPS = 32767.0
WEIGHT_STEPS = 2.0**17
PAD = 16
GROUP = 2


def smem():
    return pl.BlockSpec(memory_space=pltpu.SMEM)


def vmem():
    return pl.BlockSpec(memory_space=pltpu.VMEM)


def params(limit):
    return pltpu.CompilerParams(vmem_limit_bytes=limit * 2**20)


def bands_kernel(basis_ref, image_ref, vert_ref, horiz_ref, held_ref, arrived):
    fetches = [
        pltpu.make_async_copy(image_ref.at[s], held_ref.at[s], arrived.at[s]) for s in range(image_ref.shape[0])
    ]
    for copy in fetches:
        copy.start()
    profiles, taps = basis_ref.shape
    lead = PAD - taps // 2
    lane = lax.broadcasted_iota(jnp.int32, (8, 2 * LANE), 1)

    def body(b, _):
        down = jnp.zeros((8, 2 * LANE), f32)
        across = jnp.zeros((8, 2 * LANE), f32)
        for t in range(taps):
            down = jnp.where(lane == lead + t, basis_ref[b, t], down)
            across = jnp.where(lane == 2 * LANE - lead - t, basis_ref[b, t], across)
        for base in range(0, 2 * LANE, 16):
            if base < LANE:
                halves = [pltpu.roll(down, base + 8 * h, 1, stride=1, stride_axis=0) for h in range(2)]
                vert_ref[b, base : base + 16, :] = jnp.concatenate(halves, axis=0).astype(bf16)
            halves = [pltpu.roll(across, base + 8 * h, 1, stride=1, stride_axis=0) for h in range(2)]
            horiz_ref[b, base : base + 16, :] = jnp.concatenate(halves, axis=0)[:, :LANE].astype(bf16)
        return 0

    lax.fori_loop(0, profiles, body, 0)
    for copy in fetches:
        copy.wait()


def tap_bands(basis, images):
    profiles = basis.shape[0]
    return pl.pallas_call(
        bands_kernel,
        out_shape=(
            jax.ShapeDtypeStruct((profiles, LANE, 2 * LANE), bf16),
            jax.ShapeDtypeStruct((profiles, 2 * LANE, LANE), bf16),
            jax.ShapeDtypeStruct(images.shape, bf16),
        ),
        in_specs=[smem(), pl.BlockSpec(memory_space=pl.ANY)],
        out_specs=(vmem(), vmem(), vmem()),
        scratch_shapes=[pltpu.SemaphoreType.DMA((images.shape[0],))],
        compiler_params=params(38),
        name="tap_bands",
    )(basis, images)


def pack(parts, weight_word, out_ref, base):
    top = jnp.abs(parts[0])
    for part in parts[1:]:
        top = jnp.maximum(top, jnp.abs(part))
    exponent = jnp.ceil(jnp.log2(jnp.maximum(top, 1e-30)) + 0.002)
    factor = STEPS / jnp.exp2(exponent)
    words = [jnp.round(part * factor).astype(jnp.int32) for part in parts]
    half = len(parts) // 2
    for i in range(half):
        out_ref[base + 8 * i : base + 8 * i + 8, :] = (words[half + i] << 16) | (words[i] & 0xFFFF)
    out_ref[base + 8 * half : base + 8 * half + 8, :] = weight_word + (exponent.astype(jnp.int32) + 128)


def accumulate_kernel(counts_ref, weights_ref, image_ref, out_ref, held, arrived, count_ref, weight_ref, placed, *, chunk):
    slots, rows, width = image_ref.shape
    blocks, _, block, _ = held.shape
    copies = [
        pltpu.make_async_copy(image_ref.at[:, n * block : (n + 1) * block, :], held.at[n], arrived.at[n])
        for n in range(blocks)
    ]
    small = (
        pltpu.make_async_copy(counts_ref, count_ref, placed.at[0]),
        pltpu.make_async_copy(weights_ref, weight_ref, placed.at[1]),
    )
    for copy in (*small, *copies):
        copy.start()
    for copy in small:
        copy.wait()
    weights = [jnp.where(s < count_ref[0, 0], weight_ref[0, s], 0.0) for s in range(slots)]
    total = weights[0]
    for s in range(1, slots):
        total = total + weights[s]
    weight_word = jnp.round(jnp.full((8, LANE), total, f32) * WEIGHT_STEPS).astype(jnp.int32) << 8
    cols = width // LANE
    stride = (cols + 1) * 8
    for n, copy in enumerate(copies):
        copy.wait()
        for q in range(block // chunk):
            upper, lower = [], []
            for c in range(cols):
                at = slice(c * LANE, (c + 1) * LANE)
                here = slice(q * chunk, (q + 1) * chunk)
                part = held[n, 0, here, at].astype(f32) * weights[0]
                for s in range(1, slots):
                    part = part + held[n, s, here, at].astype(f32) * weights[s]
                upper.append(part[:8])
                lower.append(part[8:])
            pack(upper + lower, weight_word, out_ref, (n * (block // chunk) + q) * stride)


def accumulate(counts, weight, images, chunk=16, block=32):
    slots, rows, width = images.shape
    return pl.pallas_call(
        functools.partial(accumulate_kernel, chunk=chunk),
        out_shape=jax.ShapeDtypeStruct((rows // chunk * (width // LANE + 1) * 8, LANE), jnp.int32),
        in_specs=[pl.BlockSpec(memory_space=pl.ANY)] * 3,
        out_specs=vmem(),
        scratch_shapes=[
            pltpu.VMEM((rows // block, slots, block, width), bf16),
            pltpu.SemaphoreType.DMA((rows // block,)),
            pltpu.SMEM(counts.shape, jnp.int32),
            pltpu.SMEM(weight.shape, f32),
            pltpu.SemaphoreType.DMA((2,)),
        ],
        compiler_params=params(50),
        name="accumulate",
    )(counts, weight, images)


def share_kernel(piece_ref, out_ref):
    parts, chunk, width = out_ref.shape
    cols = width // LANE
    upper, lower, weight = [None] * cols, [None] * cols, None
    for p in range(parts):
        meta = piece_ref[p, 8 * cols :, :]
        weight = meta >> 8 if weight is None else weight + (meta >> 8)
        scale = jnp.exp2(((meta & 0xFF) - 128).astype(f32)) / STEPS
        for c in range(cols):
            word = piece_ref[p, 8 * c : 8 * c + 8, :]
            up = ((word << 16) >> 16).astype(f32) * scale
            low = (word >> 16).astype(f32) * scale
            upper[c] = up if p == 0 else upper[c] + up
            lower[c] = low if p == 0 else lower[c] + low
    weight = weight.astype(f32) / WEIGHT_STEPS
    lane = lax.broadcasted_iota(jnp.int32, (chunk, LANE), 1)
    turned = [
        pltpu.roll(jnp.concatenate([upper[c] / weight, lower[c] / weight], axis=0), PAD, 1) for c in range(cols)
    ]
    for c in range(cols):
        block = jnp.where(lane < PAD, turned[c - 1], turned[c]).astype(bf16)
        for p in range(parts):
            out_ref[p, :, c * LANE : (c + 1) * LANE] = block


def share(pieces, chunk, width):
    parts = pieces.shape[0]
    return pl.pallas_call(
        share_kernel,
        out_shape=jax.ShapeDtypeStruct((parts, chunk, width), bf16),
        in_specs=[vmem()],
        out_specs=vmem(),
        compiler_params=params(16),
        name="share",
    )(pieces)


def vertical_step(vert_ref, padded, store):
    profiles = vert_ref.shape[0]
    rows, width = padded.shape[0] - LANE, padded.shape[1]
    band = vert_ref[...].reshape(profiles * LANE, 2 * LANE)
    for n in range(rows // LANE):
        for j in range(0, width, 2 * LANE):
            at = slice(j, min(j + 2 * LANE, width))
            part = jnp.dot(band, padded[n * LANE : (n + 2) * LANE, at], preferred_element_type=f32).astype(bf16)
            for b in range(profiles):
                store(b, slice(n * LANE, (n + 1) * LANE), at, part[b * LANE : (b + 1) * LANE])


def pack_ends_kernel(turned_ref, out_ref):
    part = out_ref.shape[0]
    lane = lax.broadcasted_iota(jnp.int32, out_ref.shape, 1)
    ends = turned_ref[:part, :LANE].astype(f32)
    for n in range(1, turned_ref.shape[0] // part):
        here = pltpu.roll(turned_ref[n * part : (n + 1) * part, :LANE].astype(f32), 2 * PAD * n, 1)
        ends = jnp.where(lane < 2 * PAD * n, ends, here)
    out_ref[...] = ends.astype(bf16)


def pack_ends(turned):
    return pl.pallas_call(
        pack_ends_kernel,
        out_shape=jax.ShapeDtypeStruct((turned.shape[0] * 2 * PAD // LANE, LANE), bf16),
        grid=(1,),
        in_specs=[pl.BlockSpec((turned.shape[0], LANE), lambda i: (0, 0))],
        out_specs=pl.BlockSpec((turned.shape[0] * 2 * PAD // LANE, LANE), lambda i: (0, 0)),
        compiler_params=params(16),
        name="pack_ends",
    )(turned)


def inner_kernel(turned_ref, vert_ref, vertical_ref, padded):
    rows, width = turned_ref.shape
    padded[0:PAD, :] = jnp.zeros((PAD, width - LANE), bf16)
    padded[PAD + rows :, :] = jnp.zeros((LANE - PAD, width - LANE), bf16)
    padded[PAD : PAD + rows, :] = turned_ref[:, LANE:]

    def store(b, at, to, part):
        vertical_ref[b, at, to] = part

    vertical_step(vert_ref, padded, store)


def match_inner(turned, vert):
    rows, width = turned.shape
    return pl.pallas_call(
        inner_kernel,
        out_shape=jax.ShapeDtypeStruct((vert.shape[0], rows, width - LANE), bf16),
        in_specs=[vmem(), vmem()],
        out_specs=vmem(),
        scratch_shapes=[pltpu.VMEM((rows + LANE, width - LANE), bf16)],
        cost_estimate=pl.CostEstimate(flops=10**10, bytes_accessed=10**7, transcendentals=0),
        compiler_params=params(16),
        name="match_inner",
    )(turned, vert)


def template_kernel(turned_ref, out_ref, done_ref, template_ref, written):
    rows, width = turned_ref.shape
    cols = width // LANE
    lane = lax.broadcasted_iota(jnp.int32, (LANE, LANE), 1)
    for n in range(rows // LANE):
        at = slice(n * LANE, (n + 1) * LANE)
        back = [
            pltpu.roll(turned_ref[at, c * LANE : (c + 1) * LANE].astype(f32), LANE - PAD, 1) for c in range(cols)
        ]
        for c in range(cols):
            block = jnp.where(lane < LANE - PAD, back[c], back[(c + 1) % cols])
            template_ref[at, c * LANE : (c + 1) * LANE] = block.astype(bf16)
    copy = pltpu.make_async_copy(template_ref, out_ref, written)
    copy.start()
    done_ref[...] = jnp.zeros(done_ref.shape, f32)
    copy.wait()


def turn_back(turned):
    return pl.pallas_call(
        template_kernel,
        out_shape=(jax.ShapeDtypeStruct(turned.shape, bf16), jax.ShapeDtypeStruct((8, LANE), f32)),
        in_specs=[vmem()],
        out_specs=(pl.BlockSpec(memory_space=pl.ANY), vmem()),
        scratch_shapes=[pltpu.VMEM(turned.shape, bf16), pltpu.SemaphoreType.DMA],
        cost_estimate=pl.CostEstimate(flops=10**7, bytes_accessed=4 * 10**6, transcendentals=0),
        compiler_params=params(16),
        name="template",
    )(turned)


def match_kernel(
    count_ref,
    index_ref,
    slope_ref,
    turned_ref,
    low_ref,
    high_ref,
    vert_ref,
    horiz_ref,
    inner_ref,
    image_ref,
    _,
    diff_ref,
    padded,
    outer,
    staged,
    sent,
    *,
    group,
):
    slots, rows, width = staged.shape
    cols = width // LANE
    count = count_ref[0, 0]
    patch = lax.axis_index("patch")

    def put(s):
        return pltpu.make_async_copy(staged.at[s], diff_ref.at[s], sent.at[s])

    @pl.when(count > 0)
    def _():
        padded[0:PAD, :] = jnp.zeros((PAD, 2 * LANE), bf16)
        padded[PAD + rows :, :] = jnp.zeros((LANE - PAD, 2 * LANE), bf16)
        part = low_ref.shape[0]
        lane = lax.broadcasted_iota(jnp.int32, (part, LANE), 1)
        low = low_ref[...].astype(f32) * (patch > 0).astype(f32)
        high = high_ref[...].astype(f32) * (patch < lax.axis_size("patch") - 1).astype(f32)
        for n in range(rows // part):
            own = turned_ref[n * part : (n + 1) * part, :LANE].astype(f32)
            left = pltpu.roll(low, LANE - 2 * PAD * n, 1) if n else low
            right = pltpu.roll(high, LANE - 2 * PAD * n, 1) if n else high
            at = slice(PAD + n * part, PAD + (n + 1) * part)
            padded[at, :LANE] = jnp.where(lane < PAD, left, own).astype(bf16)
            padded[at, LANE:] = jnp.where(lane < PAD, own, right).astype(bf16)

        def store(b, at, _, part):
            outer[b, at, :] = part

        vertical_step(vert_ref, padded, store)

    center = width * lax.axis_size("patch") / 2
    column = lax.broadcasted_iota(jnp.int32, (8, LANE), 1) + patch * width

    def match_group(i, _):
        @pl.when(i * group < count)
        def _():
            for g in range(group):
                slot = i * group + g
                live = slot < count
                slope = slope_ref[0, slot]
                first, second, third = index_ref[slot, 0], index_ref[slot, 1], index_ref[slot, 2]
                bands = jnp.concatenate([horiz_ref[second], horiz_ref[third]], axis=1)
                for m in range(cols):
                    at = slice(m * LANE, (m + 1) * LANE)
                    if m == 0:
                        window = jnp.concatenate([outer[first, :, :LANE], inner_ref[first, :, :LANE]], axis=1)
                    elif m == cols - 1:
                        window = jnp.concatenate(
                            [inner_ref[first, :, width - 2 * LANE :], outer[first, :, LANE:]], axis=1
                        )
                    else:
                        window = inner_ref[first, :, (m - 1) * LANE : (m + 1) * LANE]
                    position = ((column + m * LANE).astype(f32) + 0.5 - center) / center
                    factor = (slope * position)[0:1]
                    both = jnp.dot(window, bands, preferred_element_type=f32)
                    matched = both[:, :LANE] + factor * both[:, LANE:]
                    result = jnp.where(live, image_ref[slot, :, at].astype(f32) - matched, 0.0)
                    staged[slot, :, at] = result.astype(bf16)
                put(slot).start()

        @pl.when(i * group >= count)
        def _():
            for g in range(group):
                staged[i * group + g] = jnp.zeros((rows, width), bf16)
                put(i * group + g).start()

        return 0

    lax.fori_loop(0, slots // group, match_group, 0)
    for s in range(slots):
        put(s).wait()


def match(counts, index, slopes, turned, low, high, vert, horiz, inner, images, ahead, group=GROUP):
    slots, rows, width = images.shape
    return pl.pallas_call(
        functools.partial(match_kernel, group=group),
        out_shape=jax.ShapeDtypeStruct(images.shape, bf16),
        in_specs=[smem()] * 3 + [vmem()] * 7 + [pl.BlockSpec(memory_space=pl.ANY)],
        out_specs=pl.BlockSpec(memory_space=pl.ANY),
        scratch_shapes=[
            pltpu.VMEM((rows + LANE, 2 * LANE), bf16),
            pltpu.VMEM((vert.shape[0], rows, 2 * LANE), bf16),
            pltpu.VMEM(images.shape, bf16),
            pltpu.SemaphoreType.DMA((slots,)),
        ],
        compiler_params=params(24),
        name="match",
    )(counts, index, slopes, turned, low, high, vert, horiz, inner, images, ahead)


def on_device(images, counts, slot_weight, kernel_index, kernel_slope, tap_basis):
    slots, rows, width = images.shape
    parts = lax.axis_size("epoch")
    patches = lax.axis_size("patch")
    chunk = rows // parts
    partial = accumulate(counts, slot_weight, images, chunk)
    pieces = lax.all_to_all(partial, "epoch", 0, 0, tiled=True)
    copies = share(pieces.reshape(parts, -1, LANE), chunk, width)
    turned = lax.all_to_all(copies, "epoch", 0, 0, tiled=True).reshape(rows, width)
    vert, horiz, held = tap_bands(tap_basis, images)
    ring = [(i, (i + 1) % patches) for i in range(patches)]
    ends = pack_ends(turned)
    high = lax.ppermute(ends, "patch", [(target, source) for source, target in ring])
    low = lax.ppermute(ends, "patch", ring)
    inner = match_inner(turned, vert)
    template, done = turn_back(turned)
    differences = match(
        counts, kernel_index[0], kernel_slope, turned, low, high, vert, horiz, inner, held, done
    )
    return (template, differences)


def solution(mesh):
    in_specs = (
        P("epoch", None, "patch"),
        P("patch", "epoch"),
        P("patch", "epoch"),
        P("patch", "epoch", None),
        P("patch", "epoch"),
        P(),
    )
    out_specs = (P(None, "patch"), P("epoch", None, "patch"))
    return jax.shard_map(
        on_device, mesh=mesh, in_specs=in_specs, out_specs=out_specs, check_vma=False
    )
```

```python
import functools

import jax
import jax.numpy as jnp
from jax import lax
from jax.experimental import pallas as pl
from jax.experimental.pallas import tpu as pltpu
from jax.sharding import PartitionSpec as P

f32 = jnp.float32
bf16 = jnp.bfloat16
LANE = 128
STEPS = 32767.0
WEIGHT_STEPS = 2.0**17
PAD = 16
GROUP = 2


def smem():
    return pl.BlockSpec(memory_space=pltpu.SMEM)


def vmem():
    return pl.BlockSpec(memory_space=pltpu.VMEM)


def params(limit):
    return pltpu.CompilerParams(vmem_limit_bytes=limit * 2**20)


def bands_kernel(basis_ref, vert_ref, horiz_ref):
    profiles, taps = basis_ref.shape
    lead = PAD - taps // 2
    lane = lax.broadcasted_iota(jnp.int32, (8, 2 * LANE), 1)

    def body(b, _):
        down = jnp.zeros((8, 2 * LANE), f32)
        across = jnp.zeros((8, 2 * LANE), f32)
        for t in range(taps):
            down = jnp.where(lane == lead + t, basis_ref[b, t], down)
            across = jnp.where(lane == 2 * LANE - lead - t, basis_ref[b, t], across)
        for base in range(0, 2 * LANE, 16):
            if base < LANE:
                halves = [pltpu.roll(down, base + 8 * h, 1, stride=1, stride_axis=0) for h in range(2)]
                vert_ref[b, base : base + 16, :] = jnp.concatenate(halves, axis=0).astype(bf16)
            halves = [pltpu.roll(across, base + 8 * h, 1, stride=1, stride_axis=0) for h in range(2)]
            horiz_ref[b, base : base + 16, :] = jnp.concatenate(halves, axis=0)[:, :LANE].astype(bf16)
        return 0

    lax.fori_loop(0, profiles, body, 0)


def tap_bands(basis):
    profiles = basis.shape[0]
    return pl.pallas_call(
        bands_kernel,
        out_shape=(
            jax.ShapeDtypeStruct((profiles, LANE, 2 * LANE), bf16),
            jax.ShapeDtypeStruct((profiles, 2 * LANE, LANE), bf16),
        ),
        in_specs=[smem()],
        out_specs=(vmem(), vmem()),
        compiler_params=params(38),
        name="tap_bands",
    )(basis)


def pack(parts, weight_word, out_ref, base):
    top = jnp.abs(parts[0])
    for part in parts[1:]:
        top = jnp.maximum(top, jnp.abs(part))
    exponent = jnp.ceil(jnp.log2(jnp.maximum(top, 1e-30)) + 0.002)
    factor = STEPS / jnp.exp2(exponent)
    words = [jnp.round(part * factor).astype(jnp.int32) for part in parts]
    half = len(parts) // 2
    for i in range(half):
        out_ref[base + 8 * i : base + 8 * i + 8, :] = (words[half + i] << 16) | (words[i] & 0xFFFF)
    out_ref[base + 8 * half : base + 8 * half + 8, :] = weight_word + (exponent.astype(jnp.int32) + 128)


def accumulate_kernel(counts_ref, weights_ref, image_ref, out_ref, held, arrived, count_ref, weight_ref, placed, *, chunk):
    slots, rows, width = image_ref.shape
    blocks, _, block, _ = held.shape
    copies = [
        pltpu.make_async_copy(image_ref.at[:, n * block : (n + 1) * block, :], held.at[n], arrived.at[n])
        for n in range(blocks)
    ]
    small = (
        pltpu.make_async_copy(counts_ref, count_ref, placed.at[0]),
        pltpu.make_async_copy(weights_ref, weight_ref, placed.at[1]),
    )
    for copy in (*small, *copies):
        copy.start()
    for copy in small:
        copy.wait()
    weights = [jnp.where(s < count_ref[0, 0], weight_ref[0, s], 0.0) for s in range(slots)]
    total = weights[0]
    for s in range(1, slots):
        total = total + weights[s]
    weight_word = jnp.round(jnp.full((8, LANE), total, f32) * WEIGHT_STEPS).astype(jnp.int32) << 8
    cols = width // LANE
    stride = (cols + 1) * 8
    for n, copy in enumerate(copies):
        copy.wait()
        for q in range(block // chunk):
            upper, lower = [], []
            for c in range(cols):
                at = slice(c * LANE, (c + 1) * LANE)
                here = slice(q * chunk, (q + 1) * chunk)
                part = held[n, 0, here, at].astype(f32) * weights[0]
                for s in range(1, slots):
                    part = part + held[n, s, here, at].astype(f32) * weights[s]
                upper.append(part[:8])
                lower.append(part[8:])
            pack(upper + lower, weight_word, out_ref, (n * (block // chunk) + q) * stride)


def accumulate(counts, weight, images, chunk=16, block=32):
    slots, rows, width = images.shape
    return pl.pallas_call(
        functools.partial(accumulate_kernel, chunk=chunk),
        out_shape=jax.ShapeDtypeStruct((rows // chunk * (width // LANE + 1) * 8, LANE), jnp.int32),
        in_specs=[pl.BlockSpec(memory_space=pl.ANY)] * 3,
        out_specs=vmem(),
        scratch_shapes=[
            pltpu.VMEM((rows // block, slots, block, width), bf16),
            pltpu.SemaphoreType.DMA((rows // block,)),
            pltpu.SMEM(counts.shape, jnp.int32),
            pltpu.SMEM(weight.shape, f32),
            pltpu.SemaphoreType.DMA((2,)),
        ],
        compiler_params=params(50),
        name="accumulate",
    )(counts, weight, images)


def share_kernel(piece_ref, out_ref):
    parts, chunk, width = out_ref.shape
    cols = width // LANE
    upper, lower, weight = [None] * cols, [None] * cols, None
    for p in range(parts):
        meta = piece_ref[p, 8 * cols :, :]
        weight = meta >> 8 if weight is None else weight + (meta >> 8)
        scale = jnp.exp2(((meta & 0xFF) - 128).astype(f32)) / STEPS
        for c in range(cols):
            word = piece_ref[p, 8 * c : 8 * c + 8, :]
            up = ((word << 16) >> 16).astype(f32) * scale
            low = (word >> 16).astype(f32) * scale
            upper[c] = up if p == 0 else upper[c] + up
            lower[c] = low if p == 0 else lower[c] + low
    weight = weight.astype(f32) / WEIGHT_STEPS
    lane = lax.broadcasted_iota(jnp.int32, (chunk, LANE), 1)
    turned = [
        pltpu.roll(jnp.concatenate([upper[c] / weight, lower[c] / weight], axis=0), PAD, 1) for c in range(cols)
    ]
    for c in range(cols):
        block = jnp.where(lane < PAD, turned[c - 1], turned[c]).astype(bf16)
        for p in range(parts):
            out_ref[p, :, c * LANE : (c + 1) * LANE] = block


def share(pieces, chunk, width):
    parts = pieces.shape[0]
    return pl.pallas_call(
        share_kernel,
        out_shape=jax.ShapeDtypeStruct((parts, chunk, width), bf16),
        in_specs=[vmem()],
        out_specs=vmem(),
        compiler_params=params(16),
        name="share",
    )(pieces)


def vertical_step(vert_ref, padded, store):
    profiles = vert_ref.shape[0]
    rows, width = padded.shape[0] - LANE, padded.shape[1]
    band = vert_ref[...].reshape(profiles * LANE, 2 * LANE)
    for n in range(rows // LANE):
        for j in range(0, width, 2 * LANE):
            at = slice(j, min(j + 2 * LANE, width))
            part = jnp.dot(band, padded[n * LANE : (n + 2) * LANE, at], preferred_element_type=f32).astype(bf16)
            for b in range(profiles):
                store(b, slice(n * LANE, (n + 1) * LANE), at, part[b * LANE : (b + 1) * LANE])


def pack_ends_kernel(turned_ref, out_ref):
    part = out_ref.shape[0]
    lane = lax.broadcasted_iota(jnp.int32, out_ref.shape, 1)
    ends = turned_ref[:part, :LANE].astype(f32)
    for n in range(1, turned_ref.shape[0] // part):
        here = pltpu.roll(turned_ref[n * part : (n + 1) * part, :LANE].astype(f32), 2 * PAD * n, 1)
        ends = jnp.where(lane < 2 * PAD * n, ends, here)
    out_ref[...] = ends.astype(bf16)


def pack_ends(turned):
    return pl.pallas_call(
        pack_ends_kernel,
        out_shape=jax.ShapeDtypeStruct((turned.shape[0] * 2 * PAD // LANE, LANE), bf16),
        grid=(1,),
        in_specs=[pl.BlockSpec((turned.shape[0], LANE), lambda i: (0, 0))],
        out_specs=pl.BlockSpec((turned.shape[0] * 2 * PAD // LANE, LANE), lambda i: (0, 0)),
        compiler_params=params(16),
        name="pack_ends",
    )(turned)


def inner_kernel(turned_ref, vert_ref, vertical_ref, padded):
    rows, width = turned_ref.shape
    padded[0:PAD, :] = jnp.zeros((PAD, width - LANE), bf16)
    padded[PAD + rows :, :] = jnp.zeros((LANE - PAD, width - LANE), bf16)
    padded[PAD : PAD + rows, :] = turned_ref[:, LANE:]

    def store(b, at, to, part):
        vertical_ref[b, at, to] = part

    vertical_step(vert_ref, padded, store)


def match_inner(turned, vert):
    rows, width = turned.shape
    return pl.pallas_call(
        inner_kernel,
        out_shape=jax.ShapeDtypeStruct((vert.shape[0], rows, width - LANE), bf16),
        in_specs=[vmem(), vmem()],
        out_specs=vmem(),
        scratch_shapes=[pltpu.VMEM((rows + LANE, width - LANE), bf16)],
        cost_estimate=pl.CostEstimate(flops=10**10, bytes_accessed=10**7, transcendentals=0),
        compiler_params=params(16),
        name="match_inner",
    )(turned, vert)


def template_kernel(turned_ref, out_ref, done_ref, template_ref, written):
    rows, width = turned_ref.shape
    cols = width // LANE
    lane = lax.broadcasted_iota(jnp.int32, (LANE, LANE), 1)
    for n in range(rows // LANE):
        at = slice(n * LANE, (n + 1) * LANE)
        back = [
            pltpu.roll(turned_ref[at, c * LANE : (c + 1) * LANE].astype(f32), LANE - PAD, 1) for c in range(cols)
        ]
        for c in range(cols):
            block = jnp.where(lane < LANE - PAD, back[c], back[(c + 1) % cols])
            template_ref[at, c * LANE : (c + 1) * LANE] = block.astype(bf16)
    copy = pltpu.make_async_copy(template_ref, out_ref, written)
    copy.start()
    done_ref[...] = jnp.zeros(done_ref.shape, f32)
    copy.wait()


def turn_back(turned):
    return pl.pallas_call(
        template_kernel,
        out_shape=(jax.ShapeDtypeStruct(turned.shape, bf16), jax.ShapeDtypeStruct((8, LANE), f32)),
        in_specs=[vmem()],
        out_specs=(pl.BlockSpec(memory_space=pl.ANY), vmem()),
        scratch_shapes=[pltpu.VMEM(turned.shape, bf16), pltpu.SemaphoreType.DMA],
        cost_estimate=pl.CostEstimate(flops=10**7, bytes_accessed=4 * 10**6, transcendentals=0),
        compiler_params=params(16),
        name="template",
    )(turned)


def match_kernel(
    count_ref,
    index_ref,
    slope_ref,
    turned_ref,
    low_ref,
    high_ref,
    vert_ref,
    horiz_ref,
    inner_ref,
    image_ref,
    _,
    diff_ref,
    padded,
    outer,
    staged,
    sent,
    *,
    group,
):
    slots, rows, width = staged.shape
    cols = width // LANE
    count = count_ref[0, 0]
    patch = lax.axis_index("patch")

    def put(s):
        return pltpu.make_async_copy(staged.at[s], diff_ref.at[s], sent.at[s])

    @pl.when(count > 0)
    def _():
        padded[0:PAD, :] = jnp.zeros((PAD, 2 * LANE), bf16)
        padded[PAD + rows :, :] = jnp.zeros((LANE - PAD, 2 * LANE), bf16)
        part = low_ref.shape[0]
        lane = lax.broadcasted_iota(jnp.int32, (part, LANE), 1)
        low = low_ref[...].astype(f32) * (patch > 0).astype(f32)
        high = high_ref[...].astype(f32) * (patch < lax.axis_size("patch") - 1).astype(f32)
        for n in range(rows // part):
            own = turned_ref[n * part : (n + 1) * part, :LANE].astype(f32)
            left = pltpu.roll(low, LANE - 2 * PAD * n, 1) if n else low
            right = pltpu.roll(high, LANE - 2 * PAD * n, 1) if n else high
            at = slice(PAD + n * part, PAD + (n + 1) * part)
            padded[at, :LANE] = jnp.where(lane < PAD, left, own).astype(bf16)
            padded[at, LANE:] = jnp.where(lane < PAD, own, right).astype(bf16)

        def store(b, at, _, part):
            outer[b, at, :] = part

        vertical_step(vert_ref, padded, store)

    center = width * lax.axis_size("patch") / 2
    column = lax.broadcasted_iota(jnp.int32, (8, LANE), 1) + patch * width

    def match_group(i, _):
        @pl.when(i * group < count)
        def _():
            for g in range(group):
                slot = i * group + g
                live = slot < count
                slope = slope_ref[0, slot]
                first, second, third = index_ref[slot, 0], index_ref[slot, 1], index_ref[slot, 2]
                bands = jnp.concatenate([horiz_ref[second], horiz_ref[third]], axis=1)
                for m in range(cols):
                    at = slice(m * LANE, (m + 1) * LANE)
                    if m == 0:
                        window = jnp.concatenate([outer[first, :, :LANE], inner_ref[first, :, :LANE]], axis=1)
                    elif m == cols - 1:
                        window = jnp.concatenate(
                            [inner_ref[first, :, width - 2 * LANE :], outer[first, :, LANE:]], axis=1
                        )
                    else:
                        window = inner_ref[first, :, (m - 1) * LANE : (m + 1) * LANE]
                    position = ((column + m * LANE).astype(f32) + 0.5 - center) / center
                    factor = (slope * position)[0:1]
                    both = jnp.dot(window, bands, preferred_element_type=f32)
                    matched = both[:, :LANE] + factor * both[:, LANE:]
                    result = jnp.where(live, image_ref[slot, :, at].astype(f32) - matched, 0.0)
                    staged[slot, :, at] = result.astype(bf16)
                put(slot).start()

        @pl.when(i * group >= count)
        def _():
            for g in range(group):
                staged[i * group + g] = jnp.zeros((rows, width), bf16)
                put(i * group + g).start()

        return 0

    lax.fori_loop(0, slots // group, match_group, 0)
    for s in range(slots):
        put(s).wait()


def match(counts, index, slopes, turned, low, high, vert, horiz, inner, images, ahead, group=GROUP):
    slots, rows, width = images.shape
    return pl.pallas_call(
        functools.partial(match_kernel, group=group),
        out_shape=jax.ShapeDtypeStruct(images.shape, bf16),
        in_specs=[smem()] * 3 + [vmem()] * 7 + [pl.BlockSpec(memory_space=pl.ANY)],
        out_specs=pl.BlockSpec(memory_space=pl.ANY),
        scratch_shapes=[
            pltpu.VMEM((rows + LANE, 2 * LANE), bf16),
            pltpu.VMEM((vert.shape[0], rows, 2 * LANE), bf16),
            pltpu.VMEM(images.shape, bf16),
            pltpu.SemaphoreType.DMA((slots,)),
        ],
        compiler_params=params(24),
        name="match",
    )(counts, index, slopes, turned, low, high, vert, horiz, inner, images, ahead)


def on_device(images, counts, slot_weight, kernel_index, kernel_slope, tap_basis):
    slots, rows, width = images.shape
    parts = lax.axis_size("epoch")
    patches = lax.axis_size("patch")
    chunk = rows // parts
    partial = accumulate(counts, slot_weight, images, chunk)
    pieces = lax.all_to_all(partial, "epoch", 0, 0, tiled=True)
    copies = share(pieces.reshape(parts, -1, LANE), chunk, width)
    turned = lax.all_to_all(copies, "epoch", 0, 0, tiled=True).reshape(rows, width)
    vert, horiz = tap_bands(tap_basis)
    ring = [(i, (i + 1) % patches) for i in range(patches)]
    ends = pack_ends(turned)
    high = lax.ppermute(ends, "patch", [(target, source) for source, target in ring])
    low = lax.ppermute(ends, "patch", ring)
    inner = match_inner(turned, vert)
    template, done = turn_back(turned)
    differences = match(
        counts, kernel_index[0], kernel_slope, turned, low, high, vert, horiz, inner, images, done
    )
    return (template, differences)


def solution(mesh):
    in_specs = (
        P("epoch", None, "patch"),
        P("patch", "epoch"),
        P("patch", "epoch"),
        P("patch", "epoch", None),
        P("patch", "epoch"),
        P(),
    )
    out_specs = (P(None, "patch"), P("epoch", None, "patch"))
    return jax.shard_map(
        on_device, mesh=mesh, in_specs=in_specs, out_specs=out_specs, check_vma=False
    )
```
